512 devices in a mesh: pb: 16 (over x, z_hi, core), dev: 32 (over y, z_lo).
Axes of the slice: x: 4, y: 4, z: 16 (z_hi: 2, z_lo: 8; z = z_hi * 8 + z_lo), core: 2. Of those that a mesh axis runs over, the one named last changes fastest.
Arguments:
- queries: bfloat16 [16384, 128], P(('dev', 'pb')), may hold values from -0.75 to 0.75
- documents: bfloat16 [131072, 128], P(('pb', 'dev')), may hold values from -0.75 to 0.75
- lengths: int32 [1024], P(('pb', 'dev')), may hold values from 1 to 128
- normalizers: float32 [1024, 16384], P('pb', 'dev'), may hold values from 4.5 to 7.5
- probs: float32 [512, 1024], P('dev', 'pb'), may hold values from 0.01 to 0.2
- positives: int32 [512], P('dev'), may hold values from 0 to 1023
Outputs:
- query_grad: float32 [16384, 128], P(('dev', 'pb'))
- doc_grad: float32 [131072, 128], P(('pb', 'dev'))
The draws below stay inside these ranges and needn't reach their ends.
Inputs may be any that keep to these rules, and one draw needn't show every extreme that they name: `lengths`: slots of a document at positions of its length or beyond are padding. `positives`: index of the query's paired document among all 1024.
All inputs are finite; a program needn't handle non-finite values.
Results may differ from the reference program's by a relative error of at most 0.00082.
Values may be sent and summed in bfloat16 or wider, within the bound.
No kernel may reach another device: no remote copies, remote signals or barrier semaphores. Data moves between devices by JAX's collectives and lax.ppermute only.
A program may use at most 64 MiB of HBM per device.

```python
import math
import jax
import jax.numpy as jnp
from jax import lax

E = 128
LQ = 32
LD = 128
QUERIES = 512
DOCS = 1024
QTOKENS = 16384
DTOKENS = 131072
N_DEV = 32


def place_ends(array, own_key, least, top_value):
    dims = array.shape
    spot = [jax.random.randint(jax.random.fold_in(own_key, axis), (), 0, dims[axis]) for axis in range(len(dims))]
    array = array.at[tuple(spot)].set(least)
    longest = dims.index(max(dims))
    spot[longest] = (spot[longest] + 1) % dims[longest]
    return array.at[tuple(spot)].set(top_value)


def levels(stream_key, extent, pieces, least, largest):
    loudness = 1.0
    for position, blocks in pieces:
        draws = jax.random.uniform(jax.random.fold_in(jax.random.fold_in(stream_key, 6), position), (blocks,), jnp.float32, least / len(pieces), largest / len(pieces))
        loudness = loudness * jnp.repeat(jnp.exp(draws), extent[position] // blocks).reshape((-1,) + (1,) * (len(extent) - 1 - position))
    return loudness


def gaussian(stream_key, extent, spread, reach, shards=(), kind=jnp.bfloat16):
    array = jax.random.normal(stream_key, extent, jnp.float32) * spread
    if len(shards) > 0:
        array = levels(stream_key, extent, shards, -0.22, 0.18) * array
    return jnp.clip(array, min=-reach, max=reach).astype(kind)


def setup_inputs(seed: int = 0) -> dict:
    keys = jax.random.split(jax.random.key(seed), 7)
    queries = gaussian(keys[0], (QTOKENS, E), 0.125, 0.75, ((0, 512),))
    documents = gaussian(keys[1], (DTOKENS, E), 0.125, 0.75, ((0, 512),))
    lengths = place_ends(jax.random.randint(keys[2], (DOCS,), 1, LD + 1), jax.random.fold_in(keys[2], 1), 1, LD).astype(jnp.int32)
    normalizers = jnp.clip(4.5 + 3.0 * jax.random.uniform(keys[3], (DOCS, QTOKENS), jnp.float32) ** levels(keys[3], (DOCS, QTOKENS), ((0, 16), (1, 32)), -0.2, 0.2), 4.5, 7.5)
    probs = jnp.clip(jnp.exp(math.log(0.2) - 2.9957323 * jax.random.uniform(keys[4], (QUERIES, DOCS), jnp.float32) ** levels(keys[4], (QUERIES, DOCS), ((0, 32), (1, 16)), -0.2, 0.2)), 0.01, 0.2)
    positives = place_ends(jax.random.randint(keys[5], (QUERIES,), 0, DOCS), jax.random.fold_in(keys[5], 1), 0, DOCS - 1).astype(jnp.int32)
    return {"queries": queries, "documents": documents, "lengths": lengths, "normalizers": normalizers, "probs": probs, "positives": positives}


sharpness = 10.0


def interact(query_rows, z_rows, p_cols, positive_ids, doc_rows, doc_lengths, first_doc):
    query_total = query_rows.shape[0]
    query_count = p_cols.shape[0]
    query_length = query_total // query_count
    doc_count = doc_lengths.shape[0]
    doc_length = doc_rows.shape[0] // doc_count
    scores = lax.dot_general(query_rows, doc_rows, (((1,), (1,)), ((), ())), preferred_element_type=jnp.float32)
    scores = scores.reshape(query_count, query_length, doc_count, doc_length)
    doc_ids = first_doc + jnp.arange(doc_count, dtype=jnp.int32)
    signal = p_cols - (positive_ids[:, None] == doc_ids[None, :]).astype(jnp.float32)
    present = (jnp.arange(doc_length, dtype=jnp.int32)[None, :] < doc_lengths[:, None]).astype(jnp.float32)
    z_cols = jnp.transpose(z_rows.reshape(doc_count, query_count, query_length), (1, 2, 0))
    shifted = sharpness * scores - z_cols[:, :, :, None]
    shifted = jnp.minimum(shifted, 0.0)
    weight = jnp.exp(shifted) * present[None, None] * signal[:, None, :, None]
    weight = weight.reshape(query_total, doc_count * doc_length).astype(jnp.bfloat16)
    query_part = jnp.dot(weight, doc_rows, preferred_element_type=jnp.float32)
    doc_part = lax.dot_general(weight, query_rows, (((0,), (0,)), ((), ())), preferred_element_type=jnp.float32)
    return query_part, doc_part


def reference(queries, documents, lengths, normalizers, probs, positives):
    group_count = N_DEV
    query_count = QUERIES // group_count
    token_count = query_count * LQ

    def one_group(doc_total, inputs):
        query_rows, z_rows, p_rows, positive_ids = inputs
        query_part, doc_part = interact(query_rows, z_rows, p_rows, positive_ids, documents, lengths, jnp.int32(0))
        return doc_total + doc_part, query_part

    stacked = (queries.reshape(group_count, token_count, E),
               jnp.transpose(normalizers.reshape(DOCS, group_count, token_count), (1, 0, 2)),
               probs.reshape(group_count, query_count, DOCS),
               positives.reshape(group_count, query_count))
    doc_grad, query_parts = lax.scan(one_group, jnp.zeros((DTOKENS, E), jnp.float32), stacked)
    return query_parts.reshape(QTOKENS, E), doc_grad
```

```python
import jax
import jax.numpy as jnp
from jax import lax
from jax.experimental import pallas as pl
from jax.experimental.pallas import tpu as pltpu
from jax.sharding import Mesh
from jax.sharding import PartitionSpec as P

DOC_AXES = ("x", "zh", "c")
QUERY_AXES = ("y", "zl")
RING = ("zh", "zl")

SHARPNESS = 10.0
LOG2E = 1.4426950408889634
f32, bf16 = jnp.float32, jnp.bfloat16


def tile_body(q_ref, d_ref, n_ref, qg_ref, dg_ref, w_ref):
    step = pl.program_id(0)
    docs, length = n_ref.shape[1], d_ref.shape[0] // n_ref.shape[1]
    nx, nc, nzh, _, rows, width = q_ref.shape
    tokens = nx * nc * nzh * rows
    queries = tokens // rows
    q = jnp.swapaxes(q_ref[...].reshape(nx, nc, nzh, rows, width), 1, 2).reshape(tokens, width)
    z = n_ref[0, :, :tokens] * LOG2E
    one_each = n_ref[0, :, tokens : tokens + queries]
    place = lax.broadcasted_iota(jnp.int32, (queries, tokens), 1) // rows
    spread = (place == lax.broadcasted_iota(jnp.int32, (queries, tokens), 0)).astype(f32)
    signal = jnp.dot(one_each, spread, preferred_element_type=f32, precision=lax.Precision.HIGHEST)
    for k in range(docs):
        d = d_ref[k * length : (k + 1) * length, :]
        s = lax.dot_general(d, q, (((1,), (1,)), ((), ())), preferred_element_type=f32)
        t = jnp.minimum(s * (SHARPNESS * LOG2E) - z[k : k + 1, :], 0.0)
        w_ref[k * length : (k + 1) * length, :] = (jnp.exp2(t) * signal[k : k + 1, :]).astype(bf16)
    w = w_ref[...]
    qg = lax.dot_general(w, d_ref[...], (((0,), (0,)), ((), ())), preferred_element_type=f32)
    qg = jnp.transpose(qg.reshape(nx, nzh, nc, rows, width), (2, 0, 1, 3, 4))
    qg_ref[...] = qg.reshape(qg_ref.shape)
    dg = jnp.dot(w, q, preferred_element_type=f32)

    @pl.when(step == 0)
    def _():
        dg_ref[...] = dg

    @pl.when(step > 0)
    def _():
        dg_ref[...] += dg


def tile_gradients(q, d, n):
    nx, nc, nzh, nzl, rows, width = q.shape
    slots = d.shape[0]
    tokens = nx * nc * nzh * rows
    return pl.pallas_call(
        tile_body,
        grid=(nzl,),
        in_specs=[
            pl.BlockSpec((nx, nc, nzh, 1, rows, width), lambda i: (0, 0, 0, i, 0, 0)),
            pl.BlockSpec((slots, width), lambda i: (0, 0)),
            pl.BlockSpec((1, *n.shape[1:]), lambda i: (i, 0, 0)),
        ],
        out_specs=[
            pl.BlockSpec((nc, nx, nzh, 1, rows, width), lambda i: (0, 0, 0, i, 0, 0)),
            pl.BlockSpec((slots, width), lambda i: (0, 0)),
        ],
        out_shape=[
            jax.ShapeDtypeStruct((nc, nx, nzh, nzl, rows, width), f32),
            jax.ShapeDtypeStruct((slots, width), f32),
        ],
        scratch_shapes=[pltpu.VMEM((slots, tokens), bf16)],
        name="pair_tile",
        compiler_params=pltpu.CompilerParams(vmem_limit_bytes=48 * 1024 * 1024),
        cost_estimate=pl.CostEstimate(
            flops=6 * nzl * tokens * slots * width,
            bytes_accessed=8 * nzl * tokens * width,
            transcendentals=nzl * tokens * slots,
        ),
    )(q, d, n)


def per_device(queries, documents, lengths, normalizers, probs, positives):
    ny, nzl = lax.axis_size("y"), lax.axis_size("zl")
    nx, nzh, nc = (lax.axis_size(a) for a in DOC_AXES)
    nz = nzh * nzl
    rows, width = queries.shape
    local_docs = lengths.shape[0]
    length = documents.shape[0] // local_docs
    row_docs = normalizers.shape[0]
    row_queries, row_tokens = probs.shape[0], normalizers.shape[1]

    q = lax.all_to_all(
        jnp.broadcast_to(queries, (nz, rows, width)), RING, split_axis=0, concat_axis=0, tiled=True
    )
    q = lax.all_gather(q, ("x", "c"))
    q = q.reshape(nx, nc, nzh, nzl, rows, width)

    live = (jnp.arange(length, dtype=jnp.int32)[None, :] < lengths[:, None]).reshape(-1, 1)
    d = lax.all_gather(jnp.where(live, documents, 0).astype(bf16), "y", tiled=True)

    first_doc = lax.axis_index(DOC_AXES) * row_docs
    doc_ids = first_doc + jnp.arange(row_docs, dtype=jnp.int32)
    signal = probs - (positives[:, None] == doc_ids[None, :]).astype(f32)
    pad = (-row_queries) % 128
    table = jnp.concatenate(
        [normalizers, signal.T, jnp.zeros((row_docs, pad), f32)], axis=1
    )
    table = table.reshape(ny, nzl, local_docs, row_tokens + row_queries + pad)
    table = jnp.swapaxes(table, 0, 1).reshape(nzl, ny * local_docs, -1)
    table = lax.all_to_all(table, "zl", split_axis=0, concat_axis=0, tiled=True)

    qg, dg = tile_gradients(q, d, table)

    doc_grad = lax.psum_scatter(dg, "y", scatter_dimension=0, tiled=True)
    doc_grad = jnp.where(live, doc_grad, 0.0)

    me = lax.axis_index("c")
    mine = lax.dynamic_index_in_dim(qg, me, 0, keepdims=False)
    other = lax.dynamic_index_in_dim(qg, 1 - me, 0, keepdims=False)
    mine = mine + lax.ppermute(other, "c", [(0, 1), (1, 0)])
    mine = mine.reshape(nx, nz * rows, width)
    mine = jnp.sum(lax.all_to_all(mine, "x", split_axis=0, concat_axis=0, tiled=True), axis=0)
    mine = mine.reshape(nz, rows, width)
    query_grad = jnp.sum(lax.all_to_all(mine, RING, split_axis=0, concat_axis=0, tiled=True), axis=0)
    return query_grad, doc_grad


def solution(mesh):
    split = Mesh(mesh.devices.reshape(4, 2, 2, 4, 8), ("x", "zh", "c", "y", "zl"))
    return jax.shard_map(
        per_device,
        mesh=split,
        in_specs=(
            P((*QUERY_AXES, *DOC_AXES), None),
            P((*DOC_AXES, *QUERY_AXES), None),
            P((*DOC_AXES, *QUERY_AXES)),
            P(DOC_AXES, QUERY_AXES),
            P(QUERY_AXES, DOC_AXES),
            P(QUERY_AXES),
        ),
        out_specs=(P((*QUERY_AXES, *DOC_AXES), None), P((*DOC_AXES, *QUERY_AXES), None)),
        check_vma=False,
    )
```

```python
import jax
import jax.numpy as jnp
from jax import lax
from jax.experimental import pallas as pl
from jax.experimental.pallas import tpu as pltpu
from jax.sharding import Mesh
from jax.sharding import PartitionSpec as P

DOC_AXES = ("x", "zh", "c")
QUERY_AXES = ("y", "zl")
RING = ("zh", "zl")
PLANE = ("x", "c")

SHARPNESS = 10.0
LOG2E = 1.4426950408889634
TOP = 14.0
f32, f16, bf16 = jnp.float32, jnp.float16, jnp.bfloat16


def tile_body(*refs):
    *q_refs, d_ref, n_ref, qg_ref, dg_ref, top_ref, w_ref = refs
    step = pl.program_id(0)
    docs, length = n_ref.shape[1], d_ref.shape[0] // n_ref.shape[1]
    nx, nc, _, rows, width = q_refs[0].shape
    nzh = len(q_refs)
    tokens = nx * nc * nzh * rows
    queries = tokens // rows
    q = jnp.stack([r[...].reshape(nx, nc, rows, width) for r in q_refs], axis=1)
    q = q.reshape(tokens, width)
    z = n_ref[0, :, :tokens] * LOG2E
    one_each = n_ref[0, :, tokens : tokens + queries]
    place = lax.broadcasted_iota(jnp.int32, (queries, tokens), 1) // rows
    spread = (place == lax.broadcasted_iota(jnp.int32, (queries, tokens), 0)).astype(f32)
    signal = jnp.dot(one_each, spread, preferred_element_type=f32, precision=lax.Precision.HIGHEST)
    for k in range(docs):
        d = d_ref[k * length : (k + 1) * length, :]
        s = lax.dot_general(d, q, (((1,), (1,)), ((), ())), preferred_element_type=f32)
        t = jnp.minimum(s * (SHARPNESS * LOG2E) - z[k : k + 1, :], 0.0)
        w_ref[k * length : (k + 1) * length, :] = (jnp.exp2(t) * signal[k : k + 1, :]).astype(bf16)
    w = w_ref[...]
    qg = lax.dot_general(w, d_ref[...], (((0,), (0,)), ((), ())), preferred_element_type=f32)
    here = jnp.max(jnp.abs(qg).reshape(-1, 8, width), axis=0)
    qg = jnp.swapaxes(qg.reshape(nx, nzh, nc, rows, width), 1, 2)
    qg_ref[...] = qg.reshape(qg_ref.shape)
    dg = jnp.dot(w, q, preferred_element_type=f32)

    @pl.when(step == 0)
    def _():
        dg_ref[...] = dg
        top_ref[...] = here

    @pl.when(step > 0)
    def _():
        dg_ref[...] += dg
        top_ref[...] = jnp.maximum(top_ref[...], here)

    @pl.when(step == pl.num_programs(0) - 1)
    def _():
        largest = jnp.maximum(jnp.max(top_ref[...], keepdims=True), 1e-30)
        top_ref[...] = jnp.broadcast_to(jnp.ceil(jnp.log2(largest)), top_ref.shape)


def tile_gradients(parts, d, n):
    nx, nc, nzl, rows, width = parts[0].shape
    nzh = len(parts)
    slots = d.shape[0]
    tokens = nx * nc * nzh * rows
    return pl.pallas_call(
        tile_body,
        grid=(nzl,),
        in_specs=[
            *[pl.BlockSpec((nx, nc, 1, rows, width), lambda i: (0, 0, i, 0, 0))] * nzh,
            pl.BlockSpec((slots, width), lambda i: (0, 0)),
            pl.BlockSpec((1, *n.shape[1:]), lambda i: (i, 0, 0)),
        ],
        out_specs=[
            pl.BlockSpec((nx, nc, nzh, 1, rows, width), lambda i: (0, 0, 0, i, 0, 0)),
            pl.BlockSpec((slots, width), lambda i: (0, 0)),
            pl.BlockSpec((8, width), lambda i: (0, 0)),
        ],
        out_shape=[
            jax.ShapeDtypeStruct((nx, nc, nzh, nzl, rows, width), f32),
            jax.ShapeDtypeStruct((slots, width), f32),
            jax.ShapeDtypeStruct((8, width), f32),
        ],
        scratch_shapes=[pltpu.VMEM((slots, tokens), bf16)],
        name="pair_tile",
        compiler_params=pltpu.CompilerParams(vmem_limit_bytes=48 * 1024 * 1024),
        cost_estimate=pl.CostEstimate(
            flops=6 * nzl * tokens * slots * width,
            bytes_accessed=8 * nzl * tokens * width,
            transcendentals=nzl * tokens * slots,
        ),
    )(*parts, d, n)


def from_everyone(x, axes):
    copies = jnp.broadcast_to(x, (lax.axis_size(axes), *x.shape))
    return lax.all_to_all(copies, axes, split_axis=0, concat_axis=0, tiled=True)


def summed_pieces(pieces, top, axes):
    count, _, width = pieces.shape
    sent = (pieces * jnp.exp2(TOP - top)).astype(f16)
    sent = jnp.concatenate([sent, jnp.full((count, 8, width), top, f32).astype(f16)], axis=1)
    got = lax.all_to_all(sent, axes, split_axis=0, concat_axis=0, tiled=True).astype(f32)
    tops = got[:, -8, 0]
    total = jnp.sum(got[:, :-8] * jnp.exp2(tops - TOP)[:, None, None], axis=0)
    return total, jnp.max(tops)


def per_device(queries, documents, lengths, normalizers, probs, positives):
    ny, nzl = lax.axis_size("y"), lax.axis_size("zl")
    nx, nzh, nc = (lax.axis_size(a) for a in DOC_AXES)
    nz = nzh * nzl
    rows, width = queries.shape
    local_docs = lengths.shape[0]
    length = documents.shape[0] // local_docs
    row_docs = normalizers.shape[0]
    row_queries, row_tokens = probs.shape[0], normalizers.shape[1]

    q = from_everyone(queries, RING)
    live = (jnp.arange(length, dtype=jnp.int32)[None, :] < lengths[:, None]).reshape(-1, 1)
    d = lax.all_gather(jnp.where(live, documents, 0).astype(bf16), "y", tiled=True)

    first_doc = lax.axis_index(DOC_AXES) * row_docs
    doc_ids = first_doc + jnp.arange(row_docs, dtype=jnp.int32)
    signal = probs - (positives[:, None] == doc_ids[None, :]).astype(f32)
    pad = (-row_queries) % 128
    table = jnp.concatenate(
        [normalizers, signal.T, jnp.zeros((row_docs, pad), f32)], axis=1
    )
    table = table.reshape(ny, nzl, local_docs, row_tokens + row_queries + pad)
    table = jnp.swapaxes(table, 0, 1).reshape(nzl, ny * local_docs, -1)
    table = lax.all_to_all(table, "zl", split_axis=0, concat_axis=0, tiled=True)

    parts = [
        lax.all_gather(half, PLANE).reshape(nx, nc, nzl, rows, width)
        for half in q.reshape(nzh, nzl, rows, width)
    ]
    qg, dg, top = tile_gradients(parts, d, table)

    doc_grad = lax.psum_scatter(dg, "y", scatter_dimension=0, tiled=True)
    doc_grad = jnp.where(live, doc_grad, 0.0)

    mine, top = summed_pieces(qg.reshape(nx * nc, nz * rows, width), top[0, 0], PLANE)
    spare = (nx * nc - 1).bit_length()
    query_grad, _ = summed_pieces(mine.reshape(nz, rows, width), top + spare, RING)
    return query_grad, doc_grad


def solution(mesh):
    split = Mesh(mesh.devices.reshape(4, 2, 2, 4, 8), ("x", "zh", "c", "y", "zl"))
    return jax.shard_map(
        per_device,
        mesh=split,
        in_specs=(
            P((*QUERY_AXES, *DOC_AXES), None),
            P((*DOC_AXES, *QUERY_AXES), None),
            P((*DOC_AXES, *QUERY_AXES)),
            P(DOC_AXES, QUERY_AXES),
            P(QUERY_AXES, DOC_AXES),
            P(QUERY_AXES),
        ),
        out_specs=(P((*QUERY_AXES, *DOC_AXES), None), P((*DOC_AXES, *QUERY_AXES), None)),
        check_vma=False,
    )
```

```python
import jax
import jax.numpy as jnp
from jax import lax
from jax.experimental import pallas as pl
from jax.experimental.pallas import tpu as pltpu
from jax.sharding import Mesh
from jax.sharding import PartitionSpec as P

DOC_AXES = ("x", "zh", "c")
QUERY_AXES = ("y", "zl")
RING = ("zh", "zl")

SHARPNESS = 10.0
LOG2E = 1.4426950408889634
TOP = 14.0
EXPONENT_ROWS = 8
f32, f16, bf16 = jnp.float32, jnp.float16, jnp.bfloat16
HIGHEST = lax.Precision.HIGHEST


def pick(flag, one, two):
    return jnp.where(flag, one, two)


def table_body(nx, nzh, nc, ny, nzl, positives_ref, lengths_ref, z_ref, probs_ref, docs_ref, mine_ref, other_ref, d_ref, t_ref):
    row_docs, row_tokens = z_ref.shape
    row_queries = probs_ref.shape[0]
    rows = row_tokens // row_queries
    local_docs = row_docs // (ny * nzl)
    groups = row_queries // nc
    half = groups * rows
    me = lax.axis_index("c")
    first_doc = ((lax.axis_index("x") * nzh + lax.axis_index("zh")) * nc + me) * row_docs
    doc = first_doc + lax.broadcasted_iota(jnp.int32, probs_ref.shape, 1)
    query = lax.broadcasted_iota(jnp.int32, probs_ref.shape, 0)
    hit = jnp.zeros(probs_ref.shape, jnp.bool_)
    for i in range(row_queries):
        hit = hit | ((query == i) & (doc == positives_ref[i]))
    signal = probs_ref[...] - hit.astype(f32)

    z = z_ref[...] * LOG2E
    by_core = []
    for c in range(nc):
        columns = [z[:, (g * nc + c) * rows : (g * nc + c + 1) * rows] for g in range(groups)]
        one = (
            lax.broadcasted_iota(jnp.int32, (row_queries, 128), 0)
            == lax.broadcasted_iota(jnp.int32, (row_queries, 128), 1) * nc + c
        )
        turned = lax.dot_general(
            signal, one.astype(f32), (((0,), (0,)), ((), ())), preferred_element_type=f32, precision=HIGHEST
        )
        by_core.append((jnp.concatenate(columns, axis=1), turned))
    for out_ref, core in ((mine_ref, me), (other_ref, 1 - me)):
        for k in range(half // 128):
            t_ref[k] = pick(core == 0, *[b[0][:, k * 128 : (k + 1) * 128] for b in by_core])
        t_ref[half // 128] = pick(core == 0, by_core[0][1], by_core[1][1])
        tail = jnp.zeros((row_docs // local_docs, 128), f32)
        for e in range(local_docs):
            lines = [
                t_ref.at[k][pl.ds(e, row_docs // local_docs, stride=local_docs), :]
                for k in range(t_ref.shape[0])
            ]
            for k in range(half // 128):
                for y in range(ny):
                    out_ref[:, y, e * half + k * 128 : e * half + (k + 1) * 128] = lines[k][y * nzl : (y + 1) * nzl]
            part = lines[-1]
            tail = tail + (pltpu.roll(part, e * groups, 1) if e else part)
        for y in range(ny):
            out_ref[:, y, local_docs * half :] = tail[y * nzl : (y + 1) * nzl]

    length = docs_ref.shape[0] // local_docs
    for e in range(local_docs):
        block = docs_ref[e * length : (e + 1) * length, :].astype(f32)
        live = lax.broadcasted_iota(jnp.int32, block.shape, 0) < lengths_ref[e]
        d_ref[e * length : (e + 1) * length, :] = jnp.where(live, block, 0.0).astype(bf16)


def make_table(sizes, positives, lengths, normalizers, probs, documents):
    _, _, nc, ny, nzl = sizes
    row_docs, row_tokens = normalizers.shape
    half = row_tokens // nc
    local_docs = lengths.shape[0]
    shape = (nzl, ny, local_docs * half + 128)
    smem, vmem = pl.BlockSpec(memory_space=pltpu.SMEM), pl.BlockSpec(memory_space=pltpu.VMEM)
    return pl.pallas_call(
        lambda *refs: table_body(*sizes, *refs),
        in_specs=[smem, smem, vmem, vmem, vmem],
        out_specs=[vmem, vmem, vmem],
        out_shape=[
            jax.ShapeDtypeStruct(shape, f32),
            jax.ShapeDtypeStruct(shape, f32),
            jax.ShapeDtypeStruct(documents.shape, bf16),
        ],
        scratch_shapes=[pltpu.VMEM((half // 128 + 1, row_docs, 128), f32)],
        name="pair_table",
    )(positives, lengths, normalizers, probs, documents)


def tile_body(q_ref, d_ref, n_ref, qg_ref, mine_ref, other_ref, top_ref, dr_ref, w_ref):
    step = pl.program_id(0)
    ny, nc, local_slots, width = d_ref.shape
    pair, lines, _ = n_ref.shape
    nx, nzh, _, rows, _ = q_ref.shape
    groups = nx * nzh
    half = groups * rows
    tokens = pair * half
    local_docs = (n_ref.shape[2] - 128) // half
    length = local_slots // local_docs
    me = lax.axis_index("c")

    @pl.when(step == 0)
    def _():
        for r in range(nc):
            for y in range(ny):
                at = (r * ny + y) * local_slots
                dr_ref[at : at + local_slots, :] = d_ref[y, pick(r == 0, me, 1 - me)]

    q = jnp.transpose(q_ref[...], (2, 0, 1, 3, 4)).reshape(tokens, width)
    column = lax.broadcasted_iota(jnp.int32, (128, local_docs * half), 1) // rows
    spread = (column == lax.broadcasted_iota(jnp.int32, (128, local_docs * half), 0)).astype(f32)
    signal = jnp.dot(
        n_ref[:, :, local_docs * half :].reshape(pair * lines, 128),
        spread,
        preferred_element_type=f32,
        precision=HIGHEST,
    )
    for line in range(lines):
        for e in range(local_docs):
            at = (line * local_docs + e) * length
            here = slice(e * half, (e + 1) * half)
            d = dr_ref[at : at + length, :]
            s = lax.dot_general(d, q, (((1,), (1,)), ((), ())), preferred_element_type=f32)
            z = jnp.concatenate([n_ref[j, line : line + 1, here] for j in range(pair)], axis=1)
            p = jnp.concatenate(
                [signal[j * lines + line : j * lines + line + 1, here] for j in range(pair)], axis=1
            )
            t = jnp.minimum(s * (SHARPNESS * LOG2E) - z, 0.0)
            w_ref[at : at + length, :] = (jnp.exp2(t) * p).astype(bf16)
    w = w_ref[...]
    qg = lax.dot_general(w, dr_ref[...], (((0,), (0,)), ((), ())), preferred_element_type=f32)
    here = jnp.max(jnp.abs(qg).reshape(-1, 8, width), axis=0)
    qg = qg.reshape(pair, nx, nzh, rows, width)
    for j in range(pair):
        for x in range(nx):
            for zh in range(nzh):
                at = pl.multiple_of((zh * pl.num_programs(0) * pair + step * pair + j) * rows, rows)
                qg_ref[x, pl.ds(at, rows), :] = qg[j, x, zh]
    dg = jnp.dot(w, q, preferred_element_type=f32)
    own = mine_ref.shape[0]

    @pl.when(step == 0)
    def _():
        mine_ref[...] = dg[:own]
        other_ref[...] = dg[own:]
        top_ref[...] = here

    @pl.when(step > 0)
    def _():
        mine_ref[...] += dg[:own]
        other_ref[...] += dg[own:]
        top_ref[...] = jnp.maximum(top_ref[...], here)

    @pl.when(step == pl.num_programs(0) - 1)
    def _():
        largest = jnp.maximum(jnp.max(top_ref[...], keepdims=True), 1e-30)
        top = jnp.broadcast_to(jnp.ceil(jnp.log2(largest)), (1, width))
        piece = qg_ref.shape[1] - EXPONENT_ROWS
        factor = jnp.exp2(TOP - top)
        for x in range(nx):
            qg_ref[x, :piece, :] = qg_ref[x, :piece, :] * factor
            qg_ref[x, piece:, :] = jnp.broadcast_to(top, (EXPONENT_ROWS, width))


def tile_gradients(q, d, n):
    nx, nzh, nzl, rows, width = q.shape
    ny, nc, local_slots, _ = d.shape
    pair = 2
    slots = ny * nc * local_slots
    tokens = pair * nx * nzh * rows
    return pl.pallas_call(
        tile_body,
        grid=(nzl // pair,),
        in_specs=[
            pl.BlockSpec((nx, nzh, pair, rows, width), lambda i: (0, 0, i, 0, 0)),
            pl.BlockSpec(d.shape, lambda i: (0, 0, 0, 0)),
            pl.BlockSpec((pair, *n.shape[1:]), lambda i: (i, 0, 0)),
        ],
        out_specs=[
            pl.BlockSpec((nx, nzh * nzl * rows + EXPONENT_ROWS, width), lambda i: (0, 0, 0)),
            pl.BlockSpec((slots // nc, width), lambda i: (0, 0)),
            pl.BlockSpec((slots // nc, width), lambda i: (0, 0)),
        ],
        out_shape=[
            jax.ShapeDtypeStruct((nx, nzh * nzl * rows + EXPONENT_ROWS, width), f32),
            jax.ShapeDtypeStruct((slots // nc, width), f32),
            jax.ShapeDtypeStruct((slots // nc, width), f32),
        ],
        scratch_shapes=[
            pltpu.VMEM((8, width), f32),
            pltpu.VMEM((slots, width), bf16),
            pltpu.VMEM((slots, tokens), bf16),
        ],
        name="pair_tile",
        compiler_params=pltpu.CompilerParams(vmem_limit_bytes=48 * 1024 * 1024),
    )(q, d, n)


def exchange(x, axes):
    return lax.all_to_all(x, axes, split_axis=0, concat_axis=0, tiled=True)


def summed(sent, axes):
    got = exchange(sent, axes).astype(f32)
    tops = got[:, -EXPONENT_ROWS : 1 - EXPONENT_ROWS]
    return jnp.sum(got[:, :-EXPONENT_ROWS] * jnp.exp2(tops - TOP), axis=0), jnp.max(tops, axis=0)


def per_device(queries, documents, lengths, normalizers, probs, positives):
    sizes = tuple(lax.axis_size(a) for a in ("x", "zh", "c", "y", "zl"))
    nx, nzh, nc, ny, nzl = sizes
    nz = nzh * nzl
    rows, width = queries.shape
    length = documents.shape[0] // lengths.shape[0]

    q = exchange(jnp.broadcast_to(queries, (nz, rows, width)), RING).reshape(nz * rows, width)
    q = lax.all_gather(q, "x", tiled=True).reshape(nx, nzh, nzl, rows, width)

    mine, other, live_docs = make_table(sizes, positives, lengths, normalizers, probs, documents)
    swap = [(i, 1 - i) for i in range(nc)]
    table = jnp.concatenate([mine, lax.ppermute(other, "c", swap)], axis=1)
    table = exchange(table, "zl")
    d = lax.all_gather(live_docs, ("y", "c"), tiled=True).reshape(ny, nc, -1, width)

    qg, mine, other = tile_gradients(q, d, table)

    mine = (mine + lax.ppermute(other, "c", swap)).reshape(ny, -1, width)
    y = lax.axis_index("y")
    doc_grad = lax.dynamic_index_in_dim(mine, y, 0, keepdims=False)
    for k in range(1, ny):
        away = lax.dynamic_index_in_dim(mine, lax.rem(y + k, ny), 0, keepdims=False)
        doc_grad = doc_grad + lax.ppermute(away, "y", [(i, (i + k) % ny) for i in range(ny)])
    live = (jnp.arange(length, dtype=jnp.int32)[None, :] < lengths[:, None]).reshape(-1, 1)
    doc_grad = jnp.where(live, doc_grad, 0.0)

    total, top = summed(qg.astype(f16), "x")
    top = top + (nx - 1).bit_length()
    sent = (total * jnp.exp2(TOP - top)).reshape(nz, rows, width)
    sent = jnp.concatenate([sent, jnp.broadcast_to(top, (nz, EXPONENT_ROWS, width))], axis=1)
    query_grad, _ = summed(sent.astype(f16), RING)
    return query_grad, doc_grad


def solution(mesh):
    split = Mesh(mesh.devices.reshape(4, 2, 2, 4, 8), ("x", "zh", "c", "y", "zl"))
    return jax.shard_map(
        per_device,
        mesh=split,
        in_specs=(
            P((*QUERY_AXES, *DOC_AXES), None),
            P((*DOC_AXES, *QUERY_AXES), None),
            P((*DOC_AXES, *QUERY_AXES)),
            P(DOC_AXES, QUERY_AXES),
            P(QUERY_AXES, DOC_AXES),
            P(QUERY_AXES),
        ),
        out_specs=(P((*QUERY_AXES, *DOC_AXES), None), P((*DOC_AXES, *QUERY_AXES), None)),
        check_vma=False,
    )
```

```python
import jax
import jax.numpy as jnp
from jax import lax
from jax.experimental import pallas as pl
from jax.experimental.pallas import tpu as pltpu
from jax.sharding import Mesh
from jax.sharding import PartitionSpec as P

DOC_AXES = ("x", "zh", "c")
QUERY_AXES = ("y", "zl")
RING = ("zh", "zl")

SHARPNESS = 10.0
LOG2E = 1.4426950408889634
TOP = 14.0
EXPONENT_ROWS = 8
MIB = 1024 * 1024
f32, f16, bf16 = jnp.float32, jnp.float16, jnp.bfloat16
HIGHEST = lax.Precision.HIGHEST


def mask_body(lengths_ref, docs_ref, d_ref):
    local_docs = lengths_ref.shape[0]
    length = docs_ref.shape[0] // local_docs
    for e in range(local_docs):
        block = docs_ref[e * length : (e + 1) * length, :].astype(f32)
        live = lax.broadcasted_iota(jnp.int32, block.shape, 0) < lengths_ref[e]
        d_ref[e * length : (e + 1) * length, :] = jnp.where(live, block, 0.0).astype(bf16)


def without_padding(documents, lengths):
    smem, vmem = pl.BlockSpec(memory_space=pltpu.SMEM), pl.BlockSpec(memory_space=pltpu.VMEM)
    return pl.pallas_call(
        mask_body,
        in_specs=[smem, vmem],
        out_specs=vmem,
        out_shape=jax.ShapeDtypeStruct(documents.shape, bf16),
        name="live_documents",
        compiler_params=pltpu.CompilerParams(vmem_limit_bytes=12 * MIB),
    )(lengths, documents)


def table_body(nx, nzh, nc, ny, nzl, positives_ref, z_ref, probs_ref, after_ref, out_ref, t_ref):
    row_docs, row_tokens = z_ref.shape
    row_queries = probs_ref.shape[0]
    rows = row_tokens // row_queries
    local_docs = row_docs // (ny * nzl)
    groups = row_queries // nc
    half = groups * rows
    chunks = half // 128
    first_doc = ((lax.axis_index("x") * nzh + lax.axis_index("zh")) * nc + lax.axis_index("c")) * row_docs
    doc = first_doc + lax.broadcasted_iota(jnp.int32, probs_ref.shape, 1)
    query = lax.broadcasted_iota(jnp.int32, probs_ref.shape, 0)
    hit = jnp.zeros(probs_ref.shape, jnp.bool_)
    for i in range(row_queries):
        hit = hit | ((query == i) & (doc == positives_ref[i]))
    signal = probs_ref[...] - hit.astype(f32)

    z = z_ref[...] * LOG2E
    count = row_docs // local_docs
    for c in range(nc):
        columns = [z[:, (g * nc + c) * rows : (g * nc + c + 1) * rows] for g in range(groups)]
        columns = jnp.concatenate(columns, axis=1)
        one = (
            lax.broadcasted_iota(jnp.int32, (row_queries, 128), 0)
            == lax.broadcasted_iota(jnp.int32, (row_queries, 128), 1) * nc + c
        )
        turned = lax.dot_general(
            signal, one.astype(f32), (((0,), (0,)), ((), ())), preferred_element_type=f32, precision=HIGHEST
        )
        for k in range(chunks):
            t_ref[c, k] = columns[:, k * 128 : (k + 1) * 128]
        t_ref[c, chunks] = turned
        tail = jnp.zeros((count, 128), f32)
        for e in range(local_docs):
            lines = [t_ref.at[c, k][pl.ds(e, count, stride=local_docs), :] for k in range(chunks + 1)]
            for k in range(chunks):
                for y in range(ny):
                    at = e * half + k * 128
                    out_ref[:, c, y, at : at + 128] = lines[k][y * nzl : (y + 1) * nzl]
            tail = tail + (pltpu.roll(lines[chunks], e * groups, 1) if e else lines[chunks])
        for y in range(ny):
            out_ref[:, c, y, local_docs * half :] = tail[y * nzl : (y + 1) * nzl]


def make_table(sizes, positives, normalizers, probs, after):
    _, _, nc, ny, nzl = sizes
    row_docs, row_tokens = normalizers.shape
    half = row_tokens // nc
    local_docs = row_docs // (ny * nzl)
    smem, vmem = pl.BlockSpec(memory_space=pltpu.SMEM), pl.BlockSpec(memory_space=pltpu.VMEM)
    return pl.pallas_call(
        lambda *refs: table_body(*sizes, *refs),
        in_specs=[smem, vmem, vmem, pl.BlockSpec(memory_space=pl.ANY)],
        out_specs=vmem,
        out_shape=jax.ShapeDtypeStruct((nzl, nc, ny, local_docs * half + 128), f32),
        scratch_shapes=[pltpu.VMEM((nc, half // 128 + 1, row_docs, 128), f32)],
        name="pair_table",
        compiler_params=pltpu.CompilerParams(vmem_limit_bytes=12 * MIB),
    )(positives, normalizers, probs, after)


def tile_body(own, q_ref, d_ref, n_ref, *refs):
    prior_ref = refs[0] if own else None
    qg_ref, dg_ref, top_ref, dr_ref, w_ref = refs[1 if own else 0 :]
    step = pl.program_id(0)
    ny, nc, local_slots, width = d_ref.shape
    pair, _, lines, _ = n_ref.shape
    nx, nzh, _, rows, _ = q_ref.shape
    half = nx * nzh * rows
    tokens = pair * half
    local_docs = (n_ref.shape[3] - 128) // half
    length = local_slots // local_docs
    me = lax.axis_index("c")
    core = me if own else 1 - me

    @pl.when(step == 0)
    def _():
        for y in range(ny):
            dr_ref[y * local_slots : (y + 1) * local_slots, :] = d_ref[y, core]

    q = jnp.transpose(q_ref[...], (2, 0, 1, 3, 4)).reshape(tokens, width)
    n = [n_ref[j, core] for j in range(pair)]
    column = lax.broadcasted_iota(jnp.int32, (128, local_docs * half), 1) // rows
    spread = (column == lax.broadcasted_iota(jnp.int32, (128, local_docs * half), 0)).astype(f32)
    signal = jnp.dot(
        jnp.concatenate([v[:, local_docs * half :] for v in n], axis=0),
        spread,
        preferred_element_type=f32,
        precision=HIGHEST,
    )
    for line in range(lines):
        for e in range(local_docs):
            at = (line * local_docs + e) * length
            here = slice(e * half, (e + 1) * half)
            d = dr_ref[at : at + length, :]
            s = lax.dot_general(d, q, (((1,), (1,)), ((), ())), preferred_element_type=f32)
            z = jnp.concatenate([v[line : line + 1, here] for v in n], axis=1)
            p = jnp.concatenate(
                [signal[j * lines + line : j * lines + line + 1, here] for j in range(pair)], axis=1
            )
            t = jnp.minimum(s * (SHARPNESS * LOG2E) - z, 0.0)
            w_ref[at : at + length, :] = (jnp.exp2(t) * p).astype(bf16)
    w = w_ref[...]
    qg = lax.dot_general(w, dr_ref[...], (((0,), (0,)), ((), ())), preferred_element_type=f32)
    qg = qg.reshape(pair, nx, nzh, rows, width)
    largest = jnp.zeros((8, width), f32)
    for j in range(pair):
        for x in range(nx):
            for zh in range(nzh):
                at = pl.multiple_of((zh * pl.num_programs(0) * pair + step * pair + j) * rows, rows)
                block = qg[j, x, zh]
                if own:
                    block = block + prior_ref[x, pl.ds(at, rows), :]
                    largest = jnp.maximum(largest, jnp.max(jnp.abs(block).reshape(-1, 8, width), axis=0))
                qg_ref[x, pl.ds(at, rows), :] = block
    dg = jnp.dot(w, q, preferred_element_type=f32)

    @pl.when(step == 0)
    def _():
        dg_ref[...] = dg
        top_ref[...] = largest

    @pl.when(step > 0)
    def _():
        dg_ref[...] += dg
        top_ref[...] = jnp.maximum(top_ref[...], largest)


def tile_gradients(q, d, n, prior=None):
    nx, nzh, nzl, rows, width = q.shape
    ny, nc, local_slots, _ = d.shape
    pair = 2
    slots = ny * local_slots
    own = prior is not None
    piece = nzh * nzl * rows
    whole = pl.BlockSpec((nx, piece, width), lambda i: (0, 0, 0))
    return pl.pallas_call(
        lambda *refs: tile_body(own, *refs),
        grid=(nzl // pair,),
        in_specs=[
            pl.BlockSpec((nx, nzh, pair, rows, width), lambda i: (0, 0, i, 0, 0)),
            pl.BlockSpec(d.shape, lambda i: (0, 0, 0, 0)),
            pl.BlockSpec((pair, *n.shape[1:]), lambda i: (i, 0, 0, 0)),
            *([whole] if own else []),
        ],
        out_specs=[
            whole,
            pl.BlockSpec((slots, width), lambda i: (0, 0)),
            pl.BlockSpec((8, width), lambda i: (0, 0)),
        ],
        out_shape=[
            jax.ShapeDtypeStruct((nx, piece, width), f32),
            jax.ShapeDtypeStruct((slots, width), f32),
            jax.ShapeDtypeStruct((8, width), f32),
        ],
        scratch_shapes=[
            pltpu.VMEM((slots, width), bf16),
            pltpu.VMEM((slots, pair * nx * nzh * rows), bf16),
        ],
        name="own_documents" if own else "other_documents",
        compiler_params=pltpu.CompilerParams(vmem_limit_bytes=20 * MIB),
        cost_estimate=pl.CostEstimate(
            flops=6 * nx * piece * slots * width,
            bytes_accessed=8 * nx * piece * width,
            transcendentals=nx * piece * slots,
        ),
    )(q, d, n, *([prior] if own else []))


def neighbours(y, ny):
    return y + 1 - 2 * (y % 2), ny - 1 - y


def after_tile_body(ny, qg_ref, top_ref, mine_ref, other_ref, sent_ref, give_ref, keep_ref):
    nx, piece, width = qg_ref.shape
    most = jnp.maximum(jnp.max(top_ref[...], keepdims=True), 1e-30)
    top = jnp.broadcast_to(jnp.ceil(jnp.log2(most)), (1, width))
    factor = jnp.exp2(TOP - top)
    for x in range(nx):
        sent_ref[x, :piece, :] = qg_ref[x] * factor
        sent_ref[x, piece:, :] = jnp.broadcast_to(top, (EXPONENT_ROWS, width))
    block = mine_ref.shape[0] // ny
    y = lax.axis_index("y")
    first, second = neighbours(y, ny)
    for ref, owners in ((give_ref, (first, neighbours(first, ny)[1])), (keep_ref, (y, second))):
        for i, owner in enumerate(owners):
            rows = pl.ds(pl.multiple_of(owner * block, block), block)
            ref[i] = mine_ref[rows, :] + other_ref[rows, :]


def after_tile(ny, qg, top, mine, other):
    nx, piece, width = qg.shape
    block = mine.shape[0] // ny
    vmem = pl.BlockSpec(memory_space=pltpu.VMEM)
    return pl.pallas_call(
        lambda *refs: after_tile_body(ny, *refs),
        in_specs=[vmem] * 4,
        out_specs=[vmem] * 3,
        out_shape=[
            jax.ShapeDtypeStruct((nx, piece + EXPONENT_ROWS, width), f32),
            jax.ShapeDtypeStruct((2, block, width), f32),
            jax.ShapeDtypeStruct((2, block, width), f32),
        ],
        name="scale_pieces",
        compiler_params=pltpu.CompilerParams(vmem_limit_bytes=12 * MIB),
    )(qg, top, mine, other)


def after_x_body(spare, got_ref, keep_ref, came_ref, sent_ref, give_ref, own_ref):
    nx, lines, width = got_ref.shape
    nz, rows = sent_ref.shape[0], sent_ref.shape[1] - EXPONENT_ROWS
    tops = [got_ref[x, lines - EXPONENT_ROWS : lines, :][:1] for x in range(nx)]
    top = tops[0]
    for t in tops[1:]:
        top = jnp.maximum(top, t)
    top = top + spare
    factors = [jnp.exp2(t - top) for t in tops]
    for k in range(nz):
        here = slice(k * rows, (k + 1) * rows)
        total = got_ref[0, here, :] * factors[0]
        for x in range(1, nx):
            total = total + got_ref[x, here, :] * factors[x]
        sent_ref[k, :rows, :] = total
        sent_ref[k, rows:, :] = jnp.broadcast_to(top, (EXPONENT_ROWS, width))
    own_ref[...] = keep_ref[0] + came_ref[0]
    give_ref[...] = keep_ref[1] + came_ref[1]


def after_x(nz, got, keep, came):
    nx, lines, width = got.shape
    rows = (lines - EXPONENT_ROWS) // nz
    block = keep.shape[1]
    vmem = pl.BlockSpec(memory_space=pltpu.VMEM)
    return pl.pallas_call(
        lambda *refs: after_x_body(float((nx - 1).bit_length()), *refs),
        in_specs=[vmem] * 3,
        out_specs=[vmem] * 3,
        out_shape=[
            jax.ShapeDtypeStruct((nz, rows + EXPONENT_ROWS, width), f32),
            jax.ShapeDtypeStruct((block, width), f32),
            jax.ShapeDtypeStruct((block, width), f32),
        ],
        name="sum_pieces",
        compiler_params=pltpu.CompilerParams(vmem_limit_bytes=12 * MIB),
    )(got, keep, came)


def exchange(x, axes):
    return lax.all_to_all(x, axes, split_axis=0, concat_axis=0, tiled=True)


def per_device(queries, documents, lengths, normalizers, probs, positives):
    sizes = tuple(lax.axis_size(a) for a in ("x", "zh", "c", "y", "zl"))
    nx, nzh, nc, ny, nzl = sizes
    nz = nzh * nzl
    rows, width = queries.shape
    length = documents.shape[0] // lengths.shape[0]

    q = exchange(jnp.broadcast_to(queries, (nz, rows, width)), RING).reshape(nz * rows, width)
    q = lax.all_gather(q, "x", tiled=True).reshape(nx, nzh, nzl, rows, width)

    d = lax.all_gather(without_padding(documents, lengths), ("y", "c"), tiled=True)
    table = make_table(sizes, positives, normalizers, probs, d)
    table = exchange(table.reshape(nzl * nc, *table.shape[2:]), ("zl", "c")).reshape(table.shape)
    d = d.reshape(ny, nc, -1, width)

    part, other, _ = tile_gradients(q, d, table)
    other = lax.ppermute(other, "c", [(i, 1 - i) for i in range(nc)])
    qg, mine, top = tile_gradients(q, d, table, part)

    pairs = [neighbours(i, ny) for i in range(ny)]
    sent, give, keep = after_tile(ny, qg, top, mine, other)
    came = lax.ppermute(give, "y", [(i, int(p[0])) for i, p in enumerate(pairs)])
    got = exchange(sent.astype(f16), "x").astype(f32)
    sent, give, own = after_x(nz, got, keep, came)
    came = lax.ppermute(give, "y", [(i, int(p[1])) for i, p in enumerate(pairs)])
    got = exchange(sent.astype(f16), RING).astype(f32)
    tops = got[:, -EXPONENT_ROWS : 1 - EXPONENT_ROWS]
    query_grad = jnp.sum(got[:, :-EXPONENT_ROWS] * jnp.exp2(tops - TOP), axis=0)
    live = (jnp.arange(length, dtype=jnp.int32)[None, :] < lengths[:, None]).reshape(-1, 1)
    doc_grad = jnp.where(live, own + came, 0.0)
    return query_grad, doc_grad


def solution(mesh):
    split = Mesh(mesh.devices.reshape(4, 2, 2, 4, 8), ("x", "zh", "c", "y", "zl"))
    return jax.shard_map(
        per_device,
        mesh=split,
        in_specs=(
            P((*QUERY_AXES, *DOC_AXES), None),
            P((*DOC_AXES, *QUERY_AXES), None),
            P((*DOC_AXES, *QUERY_AXES)),
            P(DOC_AXES, QUERY_AXES),
            P(QUERY_AXES, DOC_AXES),
            P(QUERY_AXES),
        ),
        out_specs=(P((*QUERY_AXES, *DOC_AXES), None), P((*DOC_AXES, *QUERY_AXES), None)),
        check_vma=False,
    )
```

```python
import jax
import jax.numpy as jnp
from jax import lax
from jax.experimental import pallas as pl
from jax.experimental.pallas import tpu as pltpu
from jax.sharding import Mesh
from jax.sharding import PartitionSpec as P

DOC_AXES = ("x", "zh", "c")
QUERY_AXES = ("y", "zl")
RING = ("zh", "zl")

SHARPNESS = 10.0
LOG2E = 1.4426950408889634
TOP = 14.0
EXPONENT_ROWS = 8
MIB = 1024 * 1024
f32, f16, bf16 = jnp.float32, jnp.float16, jnp.bfloat16
HIGHEST = lax.Precision.HIGHEST


def first_body(lengths_ref, queries_ref, docs_ref, copies_ref, d_ref):
    local_docs = lengths_ref.shape[0]
    length = docs_ref.shape[0] // local_docs
    for k in range(copies_ref.shape[0]):
        copies_ref[k] = queries_ref[...]
    for e in range(local_docs):
        block = docs_ref[e * length : (e + 1) * length, :].astype(f32)
        live = lax.broadcasted_iota(jnp.int32, block.shape, 0) < lengths_ref[e]
        d_ref[e * length : (e + 1) * length, :] = jnp.where(live, block, 0.0).astype(bf16)


def first(nz, lengths, queries, documents):
    smem, vmem = pl.BlockSpec(memory_space=pltpu.SMEM), pl.BlockSpec(memory_space=pltpu.VMEM)
    return pl.pallas_call(
        first_body,
        in_specs=[smem, vmem, vmem],
        out_specs=[vmem, vmem],
        out_shape=[
            jax.ShapeDtypeStruct((nz, *queries.shape), bf16),
            jax.ShapeDtypeStruct(documents.shape, bf16),
        ],
        name="first",
    )(lengths, queries, documents)


def table_body(nx, nzh, nc, ny, nzl, positives_ref, z_ref, probs_ref, after_ref, out_ref, t_ref):
    row_docs, row_tokens = z_ref.shape
    row_queries = probs_ref.shape[0]
    rows = row_tokens // row_queries
    local_docs = row_docs // (ny * nzl)
    groups = row_queries // nc
    half = groups * rows
    chunks = half // 128
    first_doc = ((lax.axis_index("x") * nzh + lax.axis_index("zh")) * nc + lax.axis_index("c")) * row_docs
    doc = first_doc + lax.broadcasted_iota(jnp.int32, probs_ref.shape, 1)
    query = lax.broadcasted_iota(jnp.int32, probs_ref.shape, 0)
    hit = jnp.zeros(probs_ref.shape, jnp.bool_)
    for i in range(row_queries):
        hit = hit | ((query == i) & (doc == positives_ref[i]))
    signal = probs_ref[...] - hit.astype(f32)

    z = z_ref[...] * LOG2E
    count = row_docs // local_docs
    for c in range(nc):
        columns = [z[:, (g * nc + c) * rows : (g * nc + c + 1) * rows] for g in range(groups)]
        columns = jnp.concatenate(columns, axis=1)
        one = (
            lax.broadcasted_iota(jnp.int32, (row_queries, 128), 0)
            == lax.broadcasted_iota(jnp.int32, (row_queries, 128), 1) * nc + c
        )
        turned = lax.dot_general(
            signal, one.astype(f32), (((0,), (0,)), ((), ())), preferred_element_type=f32, precision=HIGHEST
        )
        for k in range(chunks):
            t_ref[c, k] = columns[:, k * 128 : (k + 1) * 128]
        t_ref[c, chunks] = turned
        tail = jnp.zeros((count, 128), f32)
        for e in range(local_docs):
            lines = [t_ref.at[c, k][pl.ds(e, count, stride=local_docs), :] for k in range(chunks + 1)]
            for k in range(chunks):
                for y in range(ny):
                    at = e * half + k * 128
                    out_ref[:, c, y, at : at + 128] = lines[k][y * nzl : (y + 1) * nzl]
            tail = tail + (pltpu.roll(lines[chunks], e * groups, 1) if e else lines[chunks])
        for y in range(ny):
            out_ref[:, c, y, local_docs * half :] = tail[y * nzl : (y + 1) * nzl]


def make_table(sizes, positives, normalizers, probs, after):
    _, _, nc, ny, nzl = sizes
    row_docs, row_tokens = normalizers.shape
    half = row_tokens // nc
    local_docs = row_docs // (ny * nzl)
    smem, vmem = pl.BlockSpec(memory_space=pltpu.SMEM), pl.BlockSpec(memory_space=pltpu.VMEM)
    return pl.pallas_call(
        lambda *refs: table_body(*sizes, *refs),
        in_specs=[smem, vmem, vmem, pl.BlockSpec(memory_space=pl.ANY)],
        out_specs=vmem,
        out_shape=jax.ShapeDtypeStruct((nzl, nc, ny, local_docs * half + 128), f32),
        scratch_shapes=[pltpu.VMEM((nc, half // 128 + 1, row_docs, 128), f32)],
        name="pair_table",
    )(positives, normalizers, probs, after)


def tile_body(q_ref, d_ref, n_ref, sent_ref, mine_ref, other_ref, top_ref, dr_ref, nr_ref, w_ref):
    step = pl.program_id(0)
    ny, nc, local_slots, width = d_ref.shape
    pair, _, _, lanes = n_ref.shape
    lines = nc * ny
    nx, nzh, _, rows, _ = q_ref.shape
    half = nx * nzh * rows
    tokens = pair * half
    local_docs = (lanes - 128) // half
    length = local_slots // local_docs
    me = lax.axis_index("c")
    cores = (me, 1 - me)

    @pl.when(step == 0)
    def _():
        for r in range(nc):
            for y in range(ny):
                at = (r * ny + y) * local_slots
                dr_ref[at : at + local_slots, :] = d_ref[y, cores[r]]

    for j in range(pair):
        for r in range(nc):
            nr_ref[j * lines + r * ny : j * lines + (r + 1) * ny, :] = n_ref[j, cores[r]]
    q = jnp.transpose(q_ref[...], (2, 0, 1, 3, 4)).reshape(tokens, width)
    column = lax.broadcasted_iota(jnp.int32, (128, local_docs * half), 1) // rows
    spread = (column == lax.broadcasted_iota(jnp.int32, (128, local_docs * half), 0)).astype(f32)
    signal = jnp.dot(
        nr_ref[:, local_docs * half :], spread, preferred_element_type=f32, precision=HIGHEST
    )
    for line in range(lines):
        for e in range(local_docs):
            at = (line * local_docs + e) * length
            here = slice(e * half, (e + 1) * half)
            d = dr_ref[at : at + length, :]
            s = lax.dot_general(d, q, (((1,), (1,)), ((), ())), preferred_element_type=f32)
            which = [j * lines + line for j in range(pair)]
            z = jnp.concatenate([nr_ref[k : k + 1, here] for k in which], axis=1)
            p = jnp.concatenate([signal[k : k + 1, here] for k in which], axis=1)
            t = jnp.minimum(s * (SHARPNESS * LOG2E) - z, 0.0)
            w_ref[at : at + length, :] = (jnp.exp2(t) * p).astype(bf16)
    w = w_ref[...]
    qg = lax.dot_general(w, dr_ref[...], (((0,), (0,)), ((), ())), preferred_element_type=f32)
    largest = jnp.max(jnp.abs(qg).reshape(-1, 8, width), axis=0)
    qg = qg.reshape(pair, nx, nzh, rows, width)
    for j in range(pair):
        for x in range(nx):
            for zh in range(nzh):
                at = pl.multiple_of((zh * pl.num_programs(0) * pair + step * pair + j) * rows, rows)
                sent_ref[x, pl.ds(at, rows), :] = qg[j, x, zh]
    dg = jnp.dot(w, q, preferred_element_type=f32)
    own = mine_ref.shape[0]

    @pl.when(step == 0)
    def _():
        mine_ref[...] = dg[:own]
        other_ref[...] = dg[own:]
        top_ref[...] = largest

    @pl.when(step > 0)
    def _():
        mine_ref[...] += dg[:own]
        other_ref[...] += dg[own:]
        top_ref[...] = jnp.maximum(top_ref[...], largest)

    @pl.when(step == pl.num_programs(0) - 1)
    def _():
        most = jnp.maximum(jnp.max(top_ref[...], keepdims=True), 1e-30)
        top = jnp.broadcast_to(jnp.ceil(jnp.log2(most)), (1, width))
        piece = sent_ref.shape[1] - EXPONENT_ROWS
        factor = jnp.exp2(TOP - top)
        for x in range(nx):
            sent_ref[x, :piece, :] = sent_ref[x, :piece, :] * factor
            sent_ref[x, piece:, :] = jnp.broadcast_to(top, (EXPONENT_ROWS, width))


def tile_gradients(q, d, n):
    nx, nzh, nzl, rows, width = q.shape
    ny, nc, local_slots, _ = d.shape
    pair = 2
    slots = ny * nc * local_slots
    piece = nzh * nzl * rows
    part = pl.BlockSpec((slots // nc, width), lambda i: (0, 0))
    return pl.pallas_call(
        tile_body,
        grid=(nzl // pair,),
        in_specs=[
            pl.BlockSpec((nx, nzh, pair, rows, width), lambda i: (0, 0, i, 0, 0)),
            pl.BlockSpec(d.shape, lambda i: (0, 0, 0, 0)),
            pl.BlockSpec((pair, *n.shape[1:]), lambda i: (i, 0, 0, 0)),
        ],
        out_specs=[pl.BlockSpec((nx, piece + EXPONENT_ROWS, width), lambda i: (0, 0, 0)), part, part],
        out_shape=[
            jax.ShapeDtypeStruct((nx, piece + EXPONENT_ROWS, width), f32),
            jax.ShapeDtypeStruct((slots // nc, width), f32),
            jax.ShapeDtypeStruct((slots // nc, width), f32),
        ],
        scratch_shapes=[
            pltpu.VMEM((8, width), f32),
            pltpu.VMEM((slots, width), bf16),
            pltpu.VMEM((pair * nc * ny, n.shape[3]), f32),
            pltpu.VMEM((slots, pair * nx * nzh * rows), bf16),
        ],
        name="pair_tile",
        compiler_params=pltpu.CompilerParams(vmem_limit_bytes=20 * MIB),
        cost_estimate=pl.CostEstimate(
            flops=6 * nx * piece * slots * width,
            bytes_accessed=8 * nx * piece * width,
            transcendentals=nx * piece * slots,
        ),
    )(q, d, n)


def neighbours(y, ny):
    return y + 1 - 2 * (y % 2), ny - 1 - y


def sum_body(spare, got_ref, sent_ref):
    nx, lines, width = got_ref.shape
    nz, rows = sent_ref.shape[0], sent_ref.shape[1] - EXPONENT_ROWS
    tops = [got_ref[x, lines - EXPONENT_ROWS : lines, :][:1] for x in range(nx)]
    top = tops[0]
    for t in tops[1:]:
        top = jnp.maximum(top, t)
    top = top + spare
    factors = [jnp.exp2(t - top) for t in tops]
    for k in range(nz):
        here = slice(k * rows, (k + 1) * rows)
        total = got_ref[0, here, :] * factors[0]
        for x in range(1, nx):
            total = total + got_ref[x, here, :] * factors[x]
        sent_ref[k, :rows, :] = total
        sent_ref[k, rows:, :] = jnp.broadcast_to(top, (EXPONENT_ROWS, width))


def sum_pieces(nz, got):
    nx, lines, width = got.shape
    rows = (lines - EXPONENT_ROWS) // nz
    vmem = pl.BlockSpec(memory_space=pltpu.VMEM)
    return pl.pallas_call(
        lambda *refs: sum_body(float((nx - 1).bit_length()), *refs),
        in_specs=[vmem],
        out_specs=vmem,
        out_shape=jax.ShapeDtypeStruct((nz, rows + EXPONENT_ROWS, width), f32),
        name="sum_pieces",
        compiler_params=pltpu.CompilerParams(vmem_limit_bytes=12 * MIB),
    )(got)


def cores_body(ny, mine_ref, other_ref, give_ref, keep_ref):
    block = mine_ref.shape[0] // ny
    y = lax.axis_index("y")
    one, two = neighbours(y, ny)
    for ref, owners in ((give_ref, (one, neighbours(one, ny)[1])), (keep_ref, (y, two))):
        for i, owner in enumerate(owners):
            here = pl.ds(pl.multiple_of(owner * block, block), block)
            ref[i] = mine_ref[here, :] + other_ref[here, :]


def cores_added(ny, mine, other):
    block, width = mine.shape[0] // ny, mine.shape[1]
    vmem = pl.BlockSpec(memory_space=pltpu.VMEM)
    half = jax.ShapeDtypeStruct((2, block, width), f32)
    return pl.pallas_call(
        lambda *refs: cores_body(ny, *refs),
        in_specs=[vmem] * 2,
        out_specs=[vmem] * 2,
        out_shape=[half, half],
        name="cores_added",
        compiler_params=pltpu.CompilerParams(vmem_limit_bytes=12 * MIB),
    )(mine, other)


def exchange(x, axes):
    return lax.all_to_all(x, axes, split_axis=0, concat_axis=0, tiled=True)


def per_device(queries, documents, lengths, normalizers, probs, positives):
    sizes = tuple(lax.axis_size(a) for a in ("x", "zh", "c", "y", "zl"))
    nx, nzh, nc, ny, nzl = sizes
    nz = nzh * nzl
    rows, width = queries.shape
    length = documents.shape[0] // lengths.shape[0]

    copies, live_docs = first(nz, lengths, queries, documents)
    q = exchange(copies, RING).reshape(nz * rows, width)
    q = lax.all_gather(q, "x", tiled=True).reshape(nx, nzh, nzl, rows, width)

    d = lax.all_gather(live_docs, ("y", "c"), tiled=True)
    table = make_table(sizes, positives, normalizers, probs, d)
    table = exchange(table.reshape(nzl * nc, *table.shape[2:]), ("zl", "c")).reshape(table.shape)
    d = d.reshape(ny, nc, -1, width)

    sent, mine, other = tile_gradients(q, d, table)

    other = lax.ppermute(other, "c", [(i, 1 - i) for i in range(nc)])
    got = exchange(sent.astype(f16), "x").astype(f32)
    got = exchange(sum_pieces(nz, got).astype(f16), RING).astype(f32)
    give, keep = cores_added(ny, mine, other)
    pairs = [neighbours(i, ny) for i in range(ny)]
    keep = keep + lax.ppermute(give, "y", [(i, p[0]) for i, p in enumerate(pairs)])
    own = keep[0] + lax.ppermute(keep[1], "y", [(i, p[1]) for i, p in enumerate(pairs)])
    tops = got[:, -EXPONENT_ROWS : 1 - EXPONENT_ROWS]
    query_grad = jnp.sum(got[:, :-EXPONENT_ROWS] * jnp.exp2(tops - TOP), axis=0)
    live = (jnp.arange(length, dtype=jnp.int32)[None, :] < lengths[:, None]).reshape(-1, 1)
    return query_grad, jnp.where(live, own, 0.0)


def solution(mesh):
    split = Mesh(mesh.devices.reshape(4, 2, 2, 4, 8), ("x", "zh", "c", "y", "zl"))
    return jax.shard_map(
        per_device,
        mesh=split,
        in_specs=(
            P((*QUERY_AXES, *DOC_AXES), None),
            P((*DOC_AXES, *QUERY_AXES), None),
            P((*DOC_AXES, *QUERY_AXES)),
            P(DOC_AXES, QUERY_AXES),
            P(QUERY_AXES, DOC_AXES),
            P(QUERY_AXES),
        ),
        out_specs=(P((*QUERY_AXES, *DOC_AXES), None), P((*DOC_AXES, *QUERY_AXES), None)),
        check_vma=False,
    )
```

```python
import jax
import jax.numpy as jnp
from jax import lax
from jax.experimental import pallas as pl
from jax.experimental.pallas import tpu as pltpu
from jax.sharding import Mesh
from jax.sharding import PartitionSpec as P

DOC_AXES = ("x", "zh", "c")
QUERY_AXES = ("y", "zl")
RING = ("zh", "zl")

SHARPNESS = 10.0
LOG2E = 1.4426950408889634
TOP = 14.0
EXPONENT_ROWS = 8
GROUP = 4
MIB = 1024 * 1024
f32, f16, bf16 = jnp.float32, jnp.float16, jnp.bfloat16
HIGHEST = lax.Precision.HIGHEST


def first_body(lengths_ref, queries_ref, docs_ref, copies_ref, d_ref):
    local_docs = lengths_ref.shape[0]
    length = docs_ref.shape[0] // local_docs
    for k in range(copies_ref.shape[0]):
        copies_ref[k] = queries_ref[...]
    for e in range(local_docs):
        block = docs_ref[e * length : (e + 1) * length, :].astype(f32)
        live = lax.broadcasted_iota(jnp.int32, block.shape, 0) < lengths_ref[e]
        d_ref[e * length : (e + 1) * length, :] = jnp.where(live, block, 0.0).astype(bf16)


def first(nz, lengths, queries, documents):
    smem, vmem = pl.BlockSpec(memory_space=pltpu.SMEM), pl.BlockSpec(memory_space=pltpu.VMEM)
    return pl.pallas_call(
        first_body,
        in_specs=[smem, vmem, vmem],
        out_specs=[vmem, vmem],
        out_shape=[
            jax.ShapeDtypeStruct((nz, *queries.shape), bf16),
            jax.ShapeDtypeStruct(documents.shape, bf16),
        ],
        name="first",
    )(lengths, queries, documents)


def table_body(nx, nzh, nc, ny, nzl, positives_ref, z_ref, probs_ref, after_ref, out_ref, t_ref):
    row_docs, row_tokens = z_ref.shape
    row_queries = probs_ref.shape[0]
    rows = row_tokens // row_queries
    local_docs = row_docs // (ny * nzl)
    groups = row_queries // nc
    half = groups * rows
    chunks = half // 128
    first_doc = ((lax.axis_index("x") * nzh + lax.axis_index("zh")) * nc + lax.axis_index("c")) * row_docs
    doc = first_doc + lax.broadcasted_iota(jnp.int32, probs_ref.shape, 1)
    query = lax.broadcasted_iota(jnp.int32, probs_ref.shape, 0)
    hit = jnp.zeros(probs_ref.shape, jnp.bool_)
    for i in range(row_queries):
        hit = hit | ((query == i) & (doc == positives_ref[i]))
    signal = probs_ref[...] - hit.astype(f32)

    z = z_ref[...] * LOG2E
    count = row_docs // local_docs
    for c in range(nc):
        columns = [z[:, (g * nc + c) * rows : (g * nc + c + 1) * rows] for g in range(groups)]
        columns = jnp.concatenate(columns, axis=1)
        one = (
            lax.broadcasted_iota(jnp.int32, (row_queries, 128), 0)
            == lax.broadcasted_iota(jnp.int32, (row_queries, 128), 1) * nc + c
        )
        turned = lax.dot_general(
            signal, one.astype(f32), (((0,), (0,)), ((), ())), preferred_element_type=f32, precision=HIGHEST
        )
        for k in range(chunks):
            t_ref[c, k] = columns[:, k * 128 : (k + 1) * 128]
        t_ref[c, chunks] = turned
        tail = jnp.zeros((count, 128), f32)
        for e in range(local_docs):
            lines = [t_ref.at[c, k][pl.ds(e, count, stride=local_docs), :] for k in range(chunks + 1)]
            for k in range(chunks):
                for y in range(ny):
                    at = e * half + k * 128
                    out_ref[:, c, y, at : at + 128] = lines[k][y * nzl : (y + 1) * nzl]
            tail = tail + (pltpu.roll(lines[chunks], e * groups, 1) if e else lines[chunks])
        for y in range(ny):
            out_ref[:, c, y, local_docs * half :] = tail[y * nzl : (y + 1) * nzl]


def make_table(sizes, positives, normalizers, probs, after):
    _, _, nc, ny, nzl = sizes
    row_docs, row_tokens = normalizers.shape
    half = row_tokens // nc
    local_docs = row_docs // (ny * nzl)
    smem, vmem = pl.BlockSpec(memory_space=pltpu.SMEM), pl.BlockSpec(memory_space=pltpu.VMEM)
    return pl.pallas_call(
        lambda *refs: table_body(*sizes, *refs),
        in_specs=[smem, vmem, vmem, pl.BlockSpec(memory_space=pl.ANY)],
        out_specs=vmem,
        out_shape=jax.ShapeDtypeStruct((nzl, nc, ny, local_docs * half + 128), f32),
        scratch_shapes=[pltpu.VMEM((nc, half // 128 + 1, row_docs, 128), f32)],
        name="pair_table",
    )(positives, normalizers, probs, after)


def tile_body(q_ref, d_ref, n_ref, sent_ref, mine_ref, other_ref, dr_ref, nr_ref, w_ref):
    ny, nc, local_slots, width = d_ref.shape
    nzl, _, _, lanes = n_ref.shape
    lines = nc * ny
    nx, nzh, _, rows, _ = q_ref.shape
    half = nx * nzh * rows
    tokens = nzl * half
    local_docs = (lanes - 128) // half
    length = local_slots // local_docs
    me = lax.axis_index("c")
    for r, core in enumerate((me, 1 - me)):
        for y in range(ny):
            at = (r * ny + y) * local_slots
            dr_ref[at : at + local_slots, :] = d_ref[y, core]
        for j in range(nzl):
            nr_ref[j * lines + r * ny : j * lines + (r + 1) * ny, :] = n_ref[j, core]
    q = jnp.transpose(q_ref[...], (2, 0, 1, 3, 4)).reshape(tokens, width)
    column = lax.broadcasted_iota(jnp.int32, (128, local_docs * half), 1) // rows
    spread = (column == lax.broadcasted_iota(jnp.int32, (128, local_docs * half), 0)).astype(f32)
    signal = jnp.dot(
        nr_ref[:, local_docs * half :], spread, preferred_element_type=f32, precision=HIGHEST
    )
    for first_doc in range(0, lines * local_docs, GROUP):
        at = first_doc * length
        d = dr_ref[at : at + GROUP * length, :]
        s = lax.dot_general(d, q, (((1,), (1,)), ((), ())), preferred_element_type=f32)
        for k in range(GROUP):
            line, e = divmod(first_doc + k, local_docs)
            here = slice(e * half, (e + 1) * half)
            which = [j * lines + line for j in range(nzl)]
            z = jnp.concatenate([nr_ref[i : i + 1, here] for i in which], axis=1)
            p = jnp.concatenate([signal[i : i + 1, here] for i in which], axis=1)
            t = jnp.minimum(s[k * length : (k + 1) * length] * (SHARPNESS * LOG2E) - z, 0.0)
            w_ref[at + k * length : at + (k + 1) * length, :] = (jnp.exp2(t) * p).astype(bf16)
    w = w_ref[...]
    qg = lax.dot_general(dr_ref[...], w, (((0,), (0,)), ((), ())), preferred_element_type=f32).T
    most = jnp.max(jnp.max(jnp.abs(qg).reshape(-1, 8, width), axis=0), keepdims=True)
    top = jnp.broadcast_to(jnp.ceil(jnp.log2(jnp.maximum(most, 1e-30))), (1, width))
    qg = (qg * jnp.exp2(TOP - top)).reshape(nzl, nx, nzh, rows, width)
    for x in range(nx):
        for j in range(nzl):
            for zh in range(nzh):
                at = (zh * nzl + j) * rows
                sent_ref[x, at : at + rows, :] = qg[j, x, zh]
        sent_ref[x, nzh * nzl * rows :, :] = jnp.broadcast_to(top, (EXPONENT_ROWS, width))
    own = mine_ref.shape[0]
    mine_ref[...] = jnp.dot(w[:own], q, preferred_element_type=f32)
    other_ref[...] = jnp.dot(w[own:], q, preferred_element_type=f32)


def tile_gradients(q, d, n):
    nx, nzh, nzl, rows, width = q.shape
    ny, nc, local_slots, _ = d.shape
    slots = ny * nc * local_slots
    piece = nzh * nzl * rows
    vmem = pl.BlockSpec(memory_space=pltpu.VMEM)
    return pl.pallas_call(
        tile_body,
        in_specs=[vmem] * 3,
        out_specs=[vmem] * 3,
        out_shape=[
            jax.ShapeDtypeStruct((nx, piece + EXPONENT_ROWS, width), f32),
            jax.ShapeDtypeStruct((slots // nc, width), f32),
            jax.ShapeDtypeStruct((slots // nc, width), f32),
        ],
        scratch_shapes=[
            pltpu.VMEM((slots, width), bf16),
            pltpu.VMEM((nzl * nc * ny, n.shape[3]), f32),
            pltpu.VMEM((slots, nx * piece), bf16),
        ],
        name="pair_tile",
        compiler_params=pltpu.CompilerParams(vmem_limit_bytes=40 * MIB),
        cost_estimate=pl.CostEstimate(
            flops=6 * nx * piece * slots * width,
            bytes_accessed=8 * nx * piece * width,
            transcendentals=nx * piece * slots,
        ),
    )(q, d, n)


def neighbours(y, ny):
    return y + 1 - 2 * (y % 2), ny - 1 - y


def sum_body(spare, got_ref, sent_ref):
    nx, lines, width = got_ref.shape
    nz, rows = sent_ref.shape[0], sent_ref.shape[1] - EXPONENT_ROWS
    tops = [got_ref[x, lines - EXPONENT_ROWS : lines, :][:1] for x in range(nx)]
    top = tops[0]
    for t in tops[1:]:
        top = jnp.maximum(top, t)
    top = top + spare
    factors = [jnp.exp2(t - top) for t in tops]
    for k in range(nz):
        here = slice(k * rows, (k + 1) * rows)
        total = got_ref[0, here, :] * factors[0]
        for x in range(1, nx):
            total = total + got_ref[x, here, :] * factors[x]
        sent_ref[k, :rows, :] = total
        sent_ref[k, rows:, :] = jnp.broadcast_to(top, (EXPONENT_ROWS, width))


def sum_pieces(nz, got):
    nx, lines, width = got.shape
    rows = (lines - EXPONENT_ROWS) // nz
    vmem = pl.BlockSpec(memory_space=pltpu.VMEM)
    return pl.pallas_call(
        lambda *refs: sum_body(float((nx - 1).bit_length()), *refs),
        in_specs=[vmem],
        out_specs=vmem,
        out_shape=jax.ShapeDtypeStruct((nz, rows + EXPONENT_ROWS, width), f32),
        name="sum_pieces",
        compiler_params=pltpu.CompilerParams(vmem_limit_bytes=12 * MIB),
    )(got)


def cores_body(ny, mine_ref, other_ref, give_ref, keep_ref):
    block = mine_ref.shape[0] // ny
    y = lax.axis_index("y")
    one, two = neighbours(y, ny)
    for ref, owners in ((give_ref, (one, neighbours(one, ny)[1])), (keep_ref, (y, two))):
        for i, owner in enumerate(owners):
            here = pl.ds(pl.multiple_of(owner * block, block), block)
            ref[i] = mine_ref[here, :] + other_ref[here, :]


def cores_added(ny, mine, other):
    block, width = mine.shape[0] // ny, mine.shape[1]
    vmem = pl.BlockSpec(memory_space=pltpu.VMEM)
    half = jax.ShapeDtypeStruct((2, block, width), f32)
    return pl.pallas_call(
        lambda *refs: cores_body(ny, *refs),
        in_specs=[vmem] * 2,
        out_specs=[vmem] * 2,
        out_shape=[half, half],
        name="cores_added",
        compiler_params=pltpu.CompilerParams(vmem_limit_bytes=12 * MIB),
    )(mine, other)


def exchange(x, axes):
    return lax.all_to_all(x, axes, split_axis=0, concat_axis=0, tiled=True)


def per_device(queries, documents, lengths, normalizers, probs, positives):
    sizes = tuple(lax.axis_size(a) for a in ("x", "zh", "c", "y", "zl"))
    nx, nzh, nc, ny, nzl = sizes
    nz = nzh * nzl
    rows, width = queries.shape
    length = documents.shape[0] // lengths.shape[0]

    copies, live_docs = first(nz, lengths, queries, documents)
    q = exchange(copies, RING).reshape(nz * rows, width)
    q = lax.all_gather(q, "x", tiled=True).reshape(nx, nzh, nzl, rows, width)

    d = lax.all_gather(live_docs, ("y", "c"), tiled=True)
    table = make_table(sizes, positives, normalizers, probs, d)
    table = exchange(table.reshape(nzl * nc, *table.shape[2:]), ("zl", "c")).reshape(table.shape)
    d = d.reshape(ny, nc, -1, width)

    sent, mine, other = tile_gradients(q, d, table)

    other = lax.ppermute(other, "c", [(i, 1 - i) for i in range(nc)])
    got = exchange(sent.astype(f16), "x").astype(f32)
    got = exchange(sum_pieces(nz, got).astype(f16), RING).astype(f32)
    give, keep = cores_added(ny, mine, other)
    pairs = [neighbours(i, ny) for i in range(ny)]
    keep = keep + lax.ppermute(give, "y", [(i, p[0]) for i, p in enumerate(pairs)])
    own = keep[0] + lax.ppermute(keep[1], "y", [(i, p[1]) for i, p in enumerate(pairs)])
    tops = got[:, -EXPONENT_ROWS : 1 - EXPONENT_ROWS]
    query_grad = jnp.sum(got[:, :-EXPONENT_ROWS] * jnp.exp2(tops - TOP), axis=0)
    live = (jnp.arange(length, dtype=jnp.int32)[None, :] < lengths[:, None]).reshape(-1, 1)
    return query_grad, jnp.where(live, own, 0.0)


def solution(mesh):
    split = Mesh(mesh.devices.reshape(4, 2, 2, 4, 8), ("x", "zh", "c", "y", "zl"))
    return jax.shard_map(
        per_device,
        mesh=split,
        in_specs=(
            P((*QUERY_AXES, *DOC_AXES), None),
            P((*DOC_AXES, *QUERY_AXES), None),
            P((*DOC_AXES, *QUERY_AXES)),
            P(DOC_AXES, QUERY_AXES),
            P(QUERY_AXES, DOC_AXES),
            P(QUERY_AXES),
        ),
        out_specs=(P((*QUERY_AXES, *DOC_AXES), None), P((*DOC_AXES, *QUERY_AXES), None)),
        check_vma=False,
    )
```

```python
import jax
import jax.numpy as jnp
from jax import lax
from jax.experimental import pallas as pl
from jax.experimental.pallas import tpu as pltpu
from jax.sharding import Mesh
from jax.sharding import PartitionSpec as P

DOC_AXES = ("x", "zh", "c")
QUERY_AXES = ("y", "zl")
RING = ("zh", "zl")

SHARPNESS = 10.0
LOG2E = 1.4426950408889634
TOP = 14.0
EXPONENT_ROWS = 8
GROUP = 4
MIB = 1024 * 1024
f32, f16, bf16 = jnp.float32, jnp.float16, jnp.bfloat16
HIGHEST = lax.Precision.HIGHEST


def first_body(lengths_ref, queries_ref, docs_ref, copies_ref, d_ref):
    local_docs = lengths_ref.shape[0]
    length = docs_ref.shape[0] // local_docs
    for k in range(copies_ref.shape[0]):
        copies_ref[k] = queries_ref[...]
    for e in range(local_docs):
        block = docs_ref[e * length : (e + 1) * length, :].astype(f32)
        live = lax.broadcasted_iota(jnp.int32, block.shape, 0) < lengths_ref[e]
        d_ref[e * length : (e + 1) * length, :] = jnp.where(live, block, 0.0).astype(bf16)


def first(nz, lengths, queries, documents):
    smem, vmem = pl.BlockSpec(memory_space=pltpu.SMEM), pl.BlockSpec(memory_space=pltpu.VMEM)
    return pl.pallas_call(
        first_body,
        in_specs=[smem, vmem, vmem],
        out_specs=[vmem, vmem],
        out_shape=[
            jax.ShapeDtypeStruct((nz, *queries.shape), bf16),
            jax.ShapeDtypeStruct(documents.shape, bf16),
        ],
        name="first",
    )(lengths, queries, documents)


def table_body(nx, nzh, nc, ny, nzl, positives_ref, z_ref, probs_ref, after_ref, out_ref, t_ref):
    row_docs, row_tokens = z_ref.shape
    row_queries = probs_ref.shape[0]
    rows = row_tokens // row_queries
    local_docs = row_docs // (ny * nzl)
    groups = row_queries // nc
    half = groups * rows
    chunks = half // 128
    first_doc = ((lax.axis_index("x") * nzh + lax.axis_index("zh")) * nc + lax.axis_index("c")) * row_docs
    doc = first_doc + lax.broadcasted_iota(jnp.int32, probs_ref.shape, 1)
    query = lax.broadcasted_iota(jnp.int32, probs_ref.shape, 0)
    hit = jnp.zeros(probs_ref.shape, jnp.bool_)
    for i in range(row_queries):
        hit = hit | ((query == i) & (doc == positives_ref[i]))
    signal = probs_ref[...] - hit.astype(f32)

    z = z_ref[...] * LOG2E
    count = row_docs // local_docs
    for c in range(nc):
        columns = [z[:, (g * nc + c) * rows : (g * nc + c + 1) * rows] for g in range(groups)]
        columns = jnp.concatenate(columns, axis=1)
        one = (
            lax.broadcasted_iota(jnp.int32, (row_queries, 128), 0)
            == lax.broadcasted_iota(jnp.int32, (row_queries, 128), 1) * nc + c
        )
        turned = lax.dot_general(
            signal, one.astype(f32), (((0,), (0,)), ((), ())), preferred_element_type=f32, precision=HIGHEST
        )
        for k in range(chunks):
            t_ref[c, k] = columns[:, k * 128 : (k + 1) * 128]
        t_ref[c, chunks] = turned
        tail = jnp.zeros((count, 128), f32)
        for e in range(local_docs):
            lines = [t_ref.at[c, k][pl.ds(e, count, stride=local_docs), :] for k in range(chunks + 1)]
            for k in range(chunks):
                for y in range(ny):
                    at = e * half + k * 128
                    out_ref[:, c, y, at : at + 128] = lines[k][y * nzl : (y + 1) * nzl]
            tail = tail + (pltpu.roll(lines[chunks], e * groups, 1) if e else lines[chunks])
        for y in range(ny):
            out_ref[:, c, y, local_docs * half :] = tail[y * nzl : (y + 1) * nzl]


def make_table(sizes, positives, normalizers, probs, after):
    _, _, nc, ny, nzl = sizes
    row_docs, row_tokens = normalizers.shape
    half = row_tokens // nc
    local_docs = row_docs // (ny * nzl)
    smem, vmem = pl.BlockSpec(memory_space=pltpu.SMEM), pl.BlockSpec(memory_space=pltpu.VMEM)
    return pl.pallas_call(
        lambda *refs: table_body(*sizes, *refs),
        in_specs=[smem, vmem, vmem, pl.BlockSpec(memory_space=pl.ANY)],
        out_specs=vmem,
        out_shape=jax.ShapeDtypeStruct((nzl, nc, ny, local_docs * half + 128), f32),
        scratch_shapes=[pltpu.VMEM((nc, half // 128 + 1, row_docs, 128), f32)],
        name="pair_table",
    )(positives, normalizers, probs, after)


def tile_body(q_ref, d_ref, n_ref, sent_ref, mine_ref, other_ref, dr_ref, nr_ref, w_ref):
    ny, nc, local_slots, width = d_ref.shape
    nzl, _, _, lanes = n_ref.shape
    lines = nc * ny
    nx, nzh, _, rows, _ = q_ref.shape
    half = nx * nzh * rows
    tokens = nzl * half
    local_docs = (lanes - 128) // half
    length = local_slots // local_docs
    me = lax.axis_index("c")
    for r, core in enumerate((me, 1 - me)):
        for y in range(ny):
            at = (r * ny + y) * local_slots
            dr_ref[at : at + local_slots, :] = d_ref[y, core]
        for j in range(nzl):
            nr_ref[j * lines + r * ny : j * lines + (r + 1) * ny, :] = n_ref[j, core]
    q = jnp.transpose(q_ref[...], (2, 0, 1, 3, 4)).reshape(tokens, width)
    column = lax.broadcasted_iota(jnp.int32, (128, local_docs * half), 1) // rows
    spread = (column == lax.broadcasted_iota(jnp.int32, (128, local_docs * half), 0)).astype(f32)
    signal = jnp.dot(
        nr_ref[:, local_docs * half :], spread, preferred_element_type=f32, precision=HIGHEST
    )
    for first_doc in range(0, lines * local_docs, GROUP):
        at = first_doc * length
        d = dr_ref[at : at + GROUP * length, :]
        s = lax.dot_general(d, q, (((1,), (1,)), ((), ())), preferred_element_type=f32)
        for k in range(GROUP):
            line, e = divmod(first_doc + k, local_docs)
            here = slice(e * half, (e + 1) * half)
            which = [j * lines + line for j in range(nzl)]
            z = jnp.concatenate([nr_ref[i : i + 1, here] for i in which], axis=1)
            p = jnp.concatenate([signal[i : i + 1, here] for i in which], axis=1)
            t = jnp.minimum(s[k * length : (k + 1) * length] * (SHARPNESS * LOG2E) - z, 0.0)
            w_ref[at + k * length : at + (k + 1) * length, :] = (jnp.exp2(t) * p).astype(bf16)
    w = w_ref[...]
    qg = lax.dot_general(dr_ref[...], w, (((0,), (0,)), ((), ())), preferred_element_type=f32).T
    most = jnp.max(jnp.max(jnp.abs(qg).reshape(-1, 8, width), axis=0), keepdims=True)
    top = jnp.broadcast_to(jnp.ceil(jnp.log2(jnp.maximum(most, 1e-30))), (1, width))
    qg = (qg * jnp.exp2(TOP - top)).reshape(nzl, nx, nzh, rows, width)
    for x in range(nx):
        for j in range(nzl):
            for zh in range(nzh):
                at = (zh * nzl + j) * rows
                sent_ref[x, at : at + rows, :] = qg[j, x, zh]
        sent_ref[x, nzh * nzl * rows :, :] = jnp.broadcast_to(top, (EXPONENT_ROWS, width))
    own = mine_ref.shape[0]
    mine_ref[...] = jnp.dot(w[:own], q, preferred_element_type=f32)
    other_ref[...] = jnp.dot(w[own:], q, preferred_element_type=f32)


def tile_gradients(q, d, n):
    nx, nzh, nzl, rows, width = q.shape
    ny, nc, local_slots, _ = d.shape
    slots = ny * nc * local_slots
    piece = nzh * nzl * rows
    vmem = pl.BlockSpec(memory_space=pltpu.VMEM)
    return pl.pallas_call(
        tile_body,
        in_specs=[vmem] * 3,
        out_specs=[vmem] * 3,
        out_shape=[
            jax.ShapeDtypeStruct((nx, piece + EXPONENT_ROWS, width), f32),
            jax.ShapeDtypeStruct((slots // nc, width), f32),
            jax.ShapeDtypeStruct((slots // nc, width), f32),
        ],
        scratch_shapes=[
            pltpu.VMEM((slots, width), bf16),
            pltpu.VMEM((nzl * nc * ny, n.shape[3]), f32),
            pltpu.VMEM((slots, nx * piece), bf16),
        ],
        name="pair_tile",
        compiler_params=pltpu.CompilerParams(vmem_limit_bytes=40 * MIB),
        cost_estimate=pl.CostEstimate(
            flops=6 * nx * piece * slots * width,
            bytes_accessed=8 * nx * piece * width,
            transcendentals=nx * piece * slots,
        ),
    )(q, d, n)


def neighbours(y, ny):
    return y + 1 - 2 * (y % 2), ny - 1 - y


def sum_body(spare, got_ref, sent_ref):
    nx, lines, width = got_ref.shape
    nz, rows = sent_ref.shape[0], sent_ref.shape[1] - EXPONENT_ROWS
    tops = [got_ref[x, lines - EXPONENT_ROWS : lines, :][:1] for x in range(nx)]
    top = tops[0]
    for t in tops[1:]:
        top = jnp.maximum(top, t)
    top = top + spare
    factors = [jnp.exp2(t - top) for t in tops]
    for k in range(nz):
        here = slice(k * rows, (k + 1) * rows)
        total = got_ref[0, here, :] * factors[0]
        for x in range(1, nx):
            total = total + got_ref[x, here, :] * factors[x]
        sent_ref[k, :rows, :] = total
        sent_ref[k, rows:, :] = jnp.broadcast_to(top, (EXPONENT_ROWS, width))


def sum_pieces(nz, got):
    nx, lines, width = got.shape
    rows = (lines - EXPONENT_ROWS) // nz
    vmem = pl.BlockSpec(memory_space=pltpu.VMEM)
    return pl.pallas_call(
        lambda *refs: sum_body(float((nx - 1).bit_length()), *refs),
        in_specs=[vmem],
        out_specs=vmem,
        out_shape=jax.ShapeDtypeStruct((nz, rows + EXPONENT_ROWS, width), f32),
        name="sum_pieces",
        compiler_params=pltpu.CompilerParams(vmem_limit_bytes=12 * MIB),
    )(got)


def scaled(blocks, out_ref):
    rows, width = blocks[0].shape
    most = jnp.max(jnp.abs(blocks[0]).reshape(-1, 8, width), axis=0)
    for b in blocks[1:]:
        most = jnp.maximum(most, jnp.max(jnp.abs(b).reshape(-1, 8, width), axis=0))
    most = jnp.maximum(jnp.max(most, keepdims=True), 1e-30)
    top = jnp.broadcast_to(jnp.ceil(jnp.log2(most)), (1, width))
    factor = jnp.exp2(TOP - top)
    for i, b in enumerate(blocks):
        out_ref[i * rows : (i + 1) * rows, :] = b * factor
    out_ref[len(blocks) * rows :, :] = jnp.broadcast_to(top, (EXPONENT_ROWS, width))


def cores_body(ny, mine_ref, other_ref, give_ref, keep_ref):
    block = mine_ref.shape[0] // ny
    y = lax.axis_index("y")
    one, two = neighbours(y, ny)

    def added(owner):
        here = pl.ds(pl.multiple_of(owner * block, block), block)
        return mine_ref[here, :] + other_ref[here, :]

    scaled([added(one), added(neighbours(one, ny)[1])], give_ref)
    keep_ref[0] = added(y)
    keep_ref[1] = added(two)


def cores_added(ny, mine, other):
    block, width = mine.shape[0] // ny, mine.shape[1]
    vmem = pl.BlockSpec(memory_space=pltpu.VMEM)
    return pl.pallas_call(
        lambda *refs: cores_body(ny, *refs),
        in_specs=[vmem] * 2,
        out_specs=[vmem] * 2,
        out_shape=[
            jax.ShapeDtypeStruct((2 * block + EXPONENT_ROWS, width), f32),
            jax.ShapeDtypeStruct((2, block, width), f32),
        ],
        name="cores_added",
        compiler_params=pltpu.CompilerParams(vmem_limit_bytes=12 * MIB),
    )(mine, other)


def neighbour_body(keep_ref, came_ref, own_ref, give_ref):
    block = keep_ref.shape[1]
    factor = jnp.exp2(came_ref[2 * block :, :][:1] - TOP)
    own_ref[...] = keep_ref[0] + came_ref[:block, :] * factor
    scaled([keep_ref[1] + came_ref[block : 2 * block, :] * factor], give_ref)


def neighbour_added(keep, came):
    _, block, width = keep.shape
    vmem = pl.BlockSpec(memory_space=pltpu.VMEM)
    return pl.pallas_call(
        neighbour_body,
        in_specs=[vmem] * 2,
        out_specs=[vmem] * 2,
        out_shape=[
            jax.ShapeDtypeStruct((block, width), f32),
            jax.ShapeDtypeStruct((block + EXPONENT_ROWS, width), f32),
        ],
        name="neighbour_added",
        compiler_params=pltpu.CompilerParams(vmem_limit_bytes=12 * MIB),
    )(keep, came)


def exchange(x, axes):
    return lax.all_to_all(x, axes, split_axis=0, concat_axis=0, tiled=True)


def per_device(queries, documents, lengths, normalizers, probs, positives):
    sizes = tuple(lax.axis_size(a) for a in ("x", "zh", "c", "y", "zl"))
    nx, nzh, nc, ny, nzl = sizes
    nz = nzh * nzl
    rows, width = queries.shape
    length = documents.shape[0] // lengths.shape[0]

    copies, live_docs = first(nz, lengths, queries, documents)
    q = exchange(copies, RING).reshape(nz * rows, width)
    q = lax.all_gather(q, "x", tiled=True).reshape(nx, nzh, nzl, rows, width)

    d = lax.all_gather(live_docs, ("y", "c"), tiled=True)
    table = make_table(sizes, positives, normalizers, probs, d)
    table = exchange(table.reshape(nzl * nc, *table.shape[2:]), ("zl", "c")).reshape(table.shape)
    d = d.reshape(ny, nc, -1, width)

    sent, mine, other = tile_gradients(q, d, table)

    other = lax.ppermute(other, "c", [(i, 1 - i) for i in range(nc)])
    got = exchange(sent.astype(f16), "x").astype(f32)
    got = exchange(sum_pieces(nz, got).astype(f16), RING).astype(f32)
    give, keep = cores_added(ny, mine, other)
    pairs = [neighbours(i, ny) for i in range(ny)]
    came = lax.ppermute(give.astype(f16), "y", [(i, p[0]) for i, p in enumerate(pairs)])
    own, give = neighbour_added(keep, came.astype(f32))
    came = lax.ppermute(give.astype(f16), "y", [(i, p[1]) for i, p in enumerate(pairs)]).astype(f32)
    own = own + came[:-EXPONENT_ROWS] * jnp.exp2(came[-EXPONENT_ROWS : 1 - EXPONENT_ROWS] - TOP)
    tops = got[:, -EXPONENT_ROWS : 1 - EXPONENT_ROWS]
    query_grad = jnp.sum(got[:, :-EXPONENT_ROWS] * jnp.exp2(tops - TOP), axis=0)
    live = (jnp.arange(length, dtype=jnp.int32)[None, :] < lengths[:, None]).reshape(-1, 1)
    return query_grad, jnp.where(live, own, 0.0)


def solution(mesh):
    split = Mesh(mesh.devices.reshape(4, 2, 2, 4, 8), ("x", "zh", "c", "y", "zl"))
    return jax.shard_map(
        per_device,
        mesh=split,
        in_specs=(
            P((*QUERY_AXES, *DOC_AXES), None),
            P((*DOC_AXES, *QUERY_AXES), None),
            P((*DOC_AXES, *QUERY_AXES)),
            P(DOC_AXES, QUERY_AXES),
            P(QUERY_AXES, DOC_AXES),
            P(QUERY_AXES),
        ),
        out_specs=(P((*QUERY_AXES, *DOC_AXES), None), P((*DOC_AXES, *QUERY_AXES), None)),
        check_vma=False,
    )
```

```python
import jax
import jax.numpy as jnp
from jax import lax
from jax.experimental import pallas as pl
from jax.experimental.pallas import tpu as pltpu
from jax.sharding import Mesh
from jax.sharding import PartitionSpec as P

DOC_AXES = ("x", "zh", "c")
QUERY_AXES = ("y", "zl")
RING = ("zh", "zl")

SHARPNESS = 10.0
LOG2E = 1.4426950408889634
TOP = 14.0
EXPONENT_ROWS = 8
GROUP = 4
MIB = 1024 * 1024
f32, f16, bf16 = jnp.float32, jnp.float16, jnp.bfloat16
HIGHEST = lax.Precision.HIGHEST


def first_body(lengths_ref, queries_ref, docs_ref, copies_ref, d_ref):
    local_docs = lengths_ref.shape[0]
    length = docs_ref.shape[0] // local_docs
    for k in range(copies_ref.shape[0]):
        copies_ref[k] = queries_ref[...]
    for e in range(local_docs):
        block = docs_ref[e * length : (e + 1) * length, :].astype(f32)
        live = lax.broadcasted_iota(jnp.int32, block.shape, 0) < lengths_ref[e]
        d_ref[e * length : (e + 1) * length, :] = jnp.where(live, block, 0.0).astype(bf16)


def first(nz, lengths, queries, documents):
    smem, vmem = pl.BlockSpec(memory_space=pltpu.SMEM), pl.BlockSpec(memory_space=pltpu.VMEM)
    return pl.pallas_call(
        first_body,
        in_specs=[smem, vmem, vmem],
        out_specs=[vmem, vmem],
        out_shape=[
            jax.ShapeDtypeStruct((nz, *queries.shape), bf16),
            jax.ShapeDtypeStruct(documents.shape, bf16),
        ],
        name="first",
    )(lengths, queries, documents)


def table_body(nx, nzh, nc, ny, nzl, positives_ref, z_ref, probs_ref, after_ref, out_ref, t_ref):
    row_docs, row_tokens = z_ref.shape
    row_queries = probs_ref.shape[0]
    rows = row_tokens // row_queries
    local_docs = row_docs // (ny * nzl)
    groups = row_queries // nc
    half = groups * rows
    chunks = half // 128
    first_doc = ((lax.axis_index("x") * nzh + lax.axis_index("zh")) * nc + lax.axis_index("c")) * row_docs
    doc = first_doc + lax.broadcasted_iota(jnp.int32, probs_ref.shape, 1)
    query = lax.broadcasted_iota(jnp.int32, probs_ref.shape, 0)
    hit = jnp.zeros(probs_ref.shape, jnp.bool_)
    for i in range(row_queries):
        hit = hit | ((query == i) & (doc == positives_ref[i]))
    signal = probs_ref[...] - hit.astype(f32)

    z = z_ref[...] * LOG2E
    count = row_docs // local_docs
    for c in range(nc):
        columns = [z[:, (g * nc + c) * rows : (g * nc + c + 1) * rows] for g in range(groups)]
        columns = jnp.concatenate(columns, axis=1)
        one = (
            lax.broadcasted_iota(jnp.int32, (row_queries, 128), 0)
            == lax.broadcasted_iota(jnp.int32, (row_queries, 128), 1) * nc + c
        )
        turned = lax.dot_general(
            signal, one.astype(f32), (((0,), (0,)), ((), ())), preferred_element_type=f32, precision=HIGHEST
        )
        for k in range(chunks):
            t_ref[c, k] = columns[:, k * 128 : (k + 1) * 128]
        t_ref[c, chunks] = turned
        tail = jnp.zeros((count, 128), f32)
        for e in range(local_docs):
            lines = [t_ref.at[c, k][pl.ds(e, count, stride=local_docs), :] for k in range(chunks + 1)]
            for k in range(chunks):
                for y in range(ny):
                    at = e * half + k * 128
                    out_ref[:, c, y, at : at + 128] = lines[k][y * nzl : (y + 1) * nzl]
            tail = tail + (pltpu.roll(lines[chunks], e * groups, 1) if e else lines[chunks])
        for y in range(ny):
            out_ref[:, c, y, local_docs * half :] = tail[y * nzl : (y + 1) * nzl]


def make_table(sizes, positives, normalizers, probs, after):
    _, _, nc, ny, nzl = sizes
    row_docs, row_tokens = normalizers.shape
    half = row_tokens // nc
    local_docs = row_docs // (ny * nzl)
    smem, vmem = pl.BlockSpec(memory_space=pltpu.SMEM), pl.BlockSpec(memory_space=pltpu.VMEM)
    return pl.pallas_call(
        lambda *refs: table_body(*sizes, *refs),
        in_specs=[smem, vmem, vmem, pl.BlockSpec(memory_space=pl.ANY)],
        out_specs=vmem,
        out_shape=jax.ShapeDtypeStruct((nzl, nc, ny, local_docs * half + 128), f32),
        scratch_shapes=[pltpu.VMEM((nc, half // 128 + 1, row_docs, 128), f32)],
        name="pair_table",
    )(positives, normalizers, probs, after)


def tile_body(q_ref, d_ref, n_ref, sent_ref, mine_ref, other_ref, dr_ref, nr_ref, w_ref):
    ny, nc, local_slots, width = d_ref.shape
    nzl, _, _, lanes = n_ref.shape
    lines = nc * ny
    nx, nzh, _, rows, _ = q_ref.shape
    half = nx * nzh * rows
    tokens = nzl * half
    local_docs = (lanes - 128) // half
    length = local_slots // local_docs
    me = lax.axis_index("c")
    for r, core in enumerate((me, 1 - me)):
        for y in range(ny):
            at = (r * ny + y) * local_slots
            dr_ref[at : at + local_slots, :] = d_ref[y, core]
        for j in range(nzl):
            nr_ref[j * lines + r * ny : j * lines + (r + 1) * ny, :] = n_ref[j, core]
    q = jnp.transpose(q_ref[...], (2, 0, 1, 3, 4)).reshape(tokens, width)
    column = lax.broadcasted_iota(jnp.int32, (128, local_docs * half), 1) // rows
    spread = (column == lax.broadcasted_iota(jnp.int32, (128, local_docs * half), 0)).astype(f32)
    signal = jnp.dot(
        nr_ref[:, local_docs * half :], spread, preferred_element_type=f32, precision=HIGHEST
    )
    for first_doc in range(0, lines * local_docs, GROUP):
        at = first_doc * length
        d = dr_ref[at : at + GROUP * length, :]
        s = lax.dot_general(d, q, (((1,), (1,)), ((), ())), preferred_element_type=f32)
        for k in range(GROUP):
            line, e = divmod(first_doc + k, local_docs)
            here = slice(e * half, (e + 1) * half)
            which = [j * lines + line for j in range(nzl)]
            z = jnp.concatenate([nr_ref[i : i + 1, here] for i in which], axis=1)
            p = jnp.concatenate([signal[i : i + 1, here] for i in which], axis=1)
            t = jnp.minimum(s[k * length : (k + 1) * length] * (SHARPNESS * LOG2E) - z, 0.0)
            w_ref[at + k * length : at + (k + 1) * length, :] = (jnp.exp2(t) * p).astype(bf16)
    w = w_ref[...]
    qg = lax.dot_general(dr_ref[...], w, (((0,), (0,)), ((), ())), preferred_element_type=f32).T
    most = jnp.max(jnp.max(jnp.abs(qg).reshape(-1, 8, width), axis=0), keepdims=True)
    top = jnp.broadcast_to(jnp.ceil(jnp.log2(jnp.maximum(most, 1e-30))), (1, width))
    qg = (qg * jnp.exp2(TOP - top)).reshape(nzl, nx, nzh, rows, width)
    for x in range(nx):
        for j in range(nzl):
            for zh in range(nzh):
                at = (zh * nzl + j) * rows
                sent_ref[x, at : at + rows, :] = qg[j, x, zh]
        sent_ref[x, nzh * nzl * rows :, :] = jnp.broadcast_to(top, (EXPONENT_ROWS, width))
    own = mine_ref.shape[0]
    mine_ref[...] = jnp.dot(w[:own], q, preferred_element_type=f32)
    other_ref[...] = jnp.dot(w[own:], q, preferred_element_type=f32)


def tile_gradients(q, d, n):
    nx, nzh, nzl, rows, width = q.shape
    ny, nc, local_slots, _ = d.shape
    slots = ny * nc * local_slots
    piece = nzh * nzl * rows
    vmem = pl.BlockSpec(memory_space=pltpu.VMEM)
    return pl.pallas_call(
        tile_body,
        in_specs=[vmem] * 3,
        out_specs=[vmem] * 3,
        out_shape=[
            jax.ShapeDtypeStruct((nx, piece + EXPONENT_ROWS, width), f32),
            jax.ShapeDtypeStruct((slots // nc, width), f32),
            jax.ShapeDtypeStruct((slots // nc, width), f32),
        ],
        scratch_shapes=[
            pltpu.VMEM((slots, width), bf16),
            pltpu.VMEM((nzl * nc * ny, n.shape[3]), f32),
            pltpu.VMEM((slots, nx * piece), bf16),
        ],
        name="pair_tile",
        compiler_params=pltpu.CompilerParams(vmem_limit_bytes=40 * MIB),
        cost_estimate=pl.CostEstimate(
            flops=6 * nx * piece * slots * width,
            bytes_accessed=8 * nx * piece * width,
            transcendentals=nx * piece * slots,
        ),
    )(q, d, n)


def cores_body(ny, mine_ref, other_ref, *refs):
    block = mine_ref.shape[0] // ny
    y = lax.axis_index("y")
    for k, ref in enumerate(refs):
        here = pl.ds(pl.multiple_of(lax.rem(y + k, ny) * block, block), block)
        ref[...] = mine_ref[here, :] + other_ref[here, :]


def cores_added(ny, mine, other):
    block, width = mine.shape[0] // ny, mine.shape[1]
    vmem = pl.BlockSpec(memory_space=pltpu.VMEM)
    return pl.pallas_call(
        lambda *refs: cores_body(ny, *refs),
        in_specs=[vmem] * 2,
        out_specs=[vmem] * ny,
        out_shape=[jax.ShapeDtypeStruct((block, width), f32)] * ny,
        name="cores_added",
        compiler_params=pltpu.CompilerParams(vmem_limit_bytes=12 * MIB),
    )(mine, other)


def sum_body(spare, lengths_ref, got_ref, *refs):
    *part_refs, sent_ref, doc_ref = refs
    nx, lines, width = got_ref.shape
    nz, rows = sent_ref.shape[0], sent_ref.shape[1] - EXPONENT_ROWS
    tops = [got_ref[x, lines - EXPONENT_ROWS : lines, :][:1] for x in range(nx)]
    top = tops[0]
    for t in tops[1:]:
        top = jnp.maximum(top, t)
    top = top + spare
    factors = [jnp.exp2(t - top) for t in tops]
    for k in range(nz):
        here = slice(k * rows, (k + 1) * rows)
        total = got_ref[0, here, :] * factors[0]
        for x in range(1, nx):
            total = total + got_ref[x, here, :] * factors[x]
        sent_ref[k, :rows, :] = total
        sent_ref[k, rows:, :] = jnp.broadcast_to(top, (EXPONENT_ROWS, width))
    local_docs = lengths_ref.shape[0]
    length = doc_ref.shape[0] // local_docs
    for e in range(local_docs):
        here = slice(e * length, (e + 1) * length)
        total = part_refs[0][here, :]
        for part in part_refs[1:]:
            total = total + part[here, :]
        live = lax.broadcasted_iota(jnp.int32, total.shape, 0) < lengths_ref[e]
        doc_ref[here, :] = jnp.where(live, total, 0.0)


def sum_pieces(nz, lengths, got, parts):
    nx, lines, width = got.shape
    rows = (lines - EXPONENT_ROWS) // nz
    smem, vmem = pl.BlockSpec(memory_space=pltpu.SMEM), pl.BlockSpec(memory_space=pltpu.VMEM)
    return pl.pallas_call(
        lambda *refs: sum_body(float((nx - 1).bit_length()), *refs),
        in_specs=[smem, *[vmem] * (1 + len(parts))],
        out_specs=[vmem, vmem],
        out_shape=[
            jax.ShapeDtypeStruct((nz, rows + EXPONENT_ROWS, width), f32),
            jax.ShapeDtypeStruct(parts[0].shape, f32),
        ],
        name="sum_pieces",
        compiler_params=pltpu.CompilerParams(vmem_limit_bytes=12 * MIB),
    )(lengths, got, *parts)


def exchange(x, axes):
    return lax.all_to_all(x, axes, split_axis=0, concat_axis=0, tiled=True)


def per_device(queries, documents, lengths, normalizers, probs, positives):
    sizes = tuple(lax.axis_size(a) for a in ("x", "zh", "c", "y", "zl"))
    nx, nzh, nc, ny, nzl = sizes
    nz = nzh * nzl
    rows, width = queries.shape

    copies, live_docs = first(nz, lengths, queries, documents)
    q = exchange(copies, RING).reshape(nz * rows, width)
    q = lax.all_gather(q, "x", tiled=True).reshape(nx, nzh, nzl, rows, width)

    d = lax.all_gather(live_docs, ("y", "c"), tiled=True)
    table = make_table(sizes, positives, normalizers, probs, d)
    table = exchange(table.reshape(nzl * nc, *table.shape[2:]), ("zl", "c")).reshape(table.shape)
    d = d.reshape(ny, nc, -1, width)

    sent, mine, other = tile_gradients(q, d, table)

    other = lax.ppermute(other, "c", [(i, 1 - i) for i in range(nc)])
    got = exchange(sent.astype(f16), "x").astype(f32)
    parts = list(cores_added(ny, mine, other))
    for k in sorted(range(1, ny), key=lambda k: -min(k, ny - k)):
        parts[k] = lax.ppermute(parts[k], "y", [(i, (i + k) % ny) for i in range(ny)])
    sent, doc_grad = sum_pieces(nz, lengths, got, parts)
    got = exchange(sent.astype(f16), RING).astype(f32)
    tops = got[:, -EXPONENT_ROWS : 1 - EXPONENT_ROWS]
    query_grad = jnp.sum(got[:, :-EXPONENT_ROWS] * jnp.exp2(tops - TOP), axis=0)
    return query_grad, doc_grad


def solution(mesh):
    split = Mesh(mesh.devices.reshape(4, 2, 2, 4, 8), ("x", "zh", "c", "y", "zl"))
    return jax.shard_map(
        per_device,
        mesh=split,
        in_specs=(
            P((*QUERY_AXES, *DOC_AXES), None),
            P((*DOC_AXES, *QUERY_AXES), None),
            P((*DOC_AXES, *QUERY_AXES)),
            P(DOC_AXES, QUERY_AXES),
            P(QUERY_AXES, DOC_AXES),
            P(QUERY_AXES),
        ),
        out_specs=(P((*QUERY_AXES, *DOC_AXES), None), P((*DOC_AXES, *QUERY_AXES), None)),
        check_vma=False,
    )
```

```python
import jax
import jax.numpy as jnp
from jax import lax
from jax.experimental import pallas as pl
from jax.experimental.pallas import tpu as pltpu
from jax.sharding import Mesh
from jax.sharding import PartitionSpec as P

DOC_AXES = ("x", "zh", "c")
QUERY_AXES = ("y", "zl")
RING = ("zh", "zl")

SHARPNESS = 10.0
LOG2E = 1.4426950408889634
TOP = 14.0
EXPONENT_ROWS = 8
GROUP = 4
MIB = 1024 * 1024
f32, f16, bf16 = jnp.float32, jnp.float16, jnp.bfloat16
HIGHEST = lax.Precision.HIGHEST


def first_body(lengths_ref, queries_ref, docs_ref, copies_ref, d_ref):
    local_docs = lengths_ref.shape[0]
    length = docs_ref.shape[0] // local_docs
    for k in range(copies_ref.shape[0]):
        copies_ref[k] = queries_ref[...]
    for e in range(local_docs):
        block = docs_ref[e * length : (e + 1) * length, :].astype(f32)
        live = lax.broadcasted_iota(jnp.int32, block.shape, 0) < lengths_ref[e]
        d_ref[e * length : (e + 1) * length, :] = jnp.where(live, block, 0.0).astype(bf16)


def first(nz, lengths, queries, documents):
    smem, vmem = pl.BlockSpec(memory_space=pltpu.SMEM), pl.BlockSpec(memory_space=pltpu.VMEM)
    return pl.pallas_call(
        first_body,
        in_specs=[smem, vmem, vmem],
        out_specs=[vmem, vmem],
        out_shape=[
            jax.ShapeDtypeStruct((nz, *queries.shape), bf16),
            jax.ShapeDtypeStruct(documents.shape, bf16),
        ],
        name="first",
    )(lengths, queries, documents)


def table_body(nx, nzh, nc, ny, nzl, positives_ref, z_ref, probs_ref, after_ref, out_ref, t_ref):
    row_docs, row_tokens = z_ref.shape
    row_queries = probs_ref.shape[0]
    rows = row_tokens // row_queries
    local_docs = row_docs // (ny * nzl)
    groups = row_queries // nc
    half = groups * rows
    chunks = half // 128
    first_doc = ((lax.axis_index("x") * nzh + lax.axis_index("zh")) * nc + lax.axis_index("c")) * row_docs
    doc = first_doc + lax.broadcasted_iota(jnp.int32, probs_ref.shape, 1)
    query = lax.broadcasted_iota(jnp.int32, probs_ref.shape, 0)
    hit = jnp.zeros(probs_ref.shape, jnp.bool_)
    for i in range(row_queries):
        hit = hit | ((query == i) & (doc == positives_ref[i]))
    signal = probs_ref[...] - hit.astype(f32)

    z = z_ref[...] * LOG2E
    count = row_docs // local_docs
    for c in range(nc):
        columns = [z[:, (g * nc + c) * rows : (g * nc + c + 1) * rows] for g in range(groups)]
        columns = jnp.concatenate(columns, axis=1)
        one = (
            lax.broadcasted_iota(jnp.int32, (row_queries, 128), 0)
            == lax.broadcasted_iota(jnp.int32, (row_queries, 128), 1) * nc + c
        )
        turned = lax.dot_general(
            signal, one.astype(f32), (((0,), (0,)), ((), ())), preferred_element_type=f32, precision=HIGHEST
        )
        for k in range(chunks):
            t_ref[c, k] = columns[:, k * 128 : (k + 1) * 128]
        t_ref[c, chunks] = turned
        tail = jnp.zeros((count, 128), f32)
        for e in range(local_docs):
            lines = [t_ref.at[c, k][pl.ds(e, count, stride=local_docs), :] for k in range(chunks + 1)]
            for k in range(chunks):
                for y in range(ny):
                    at = e * half + k * 128
                    out_ref[:, c, y, at : at + 128] = lines[k][y * nzl : (y + 1) * nzl]
            tail = tail + (pltpu.roll(lines[chunks], e * groups, 1) if e else lines[chunks])
        for y in range(ny):
            out_ref[:, c, y, local_docs * half :] = tail[y * nzl : (y + 1) * nzl]


def make_table(sizes, positives, normalizers, probs, after):
    _, _, nc, ny, nzl = sizes
    row_docs, row_tokens = normalizers.shape
    half = row_tokens // nc
    local_docs = row_docs // (ny * nzl)
    smem, vmem = pl.BlockSpec(memory_space=pltpu.SMEM), pl.BlockSpec(memory_space=pltpu.VMEM)
    return pl.pallas_call(
        lambda *refs: table_body(*sizes, *refs),
        in_specs=[smem, vmem, vmem, pl.BlockSpec(memory_space=pl.ANY)],
        out_specs=vmem,
        out_shape=jax.ShapeDtypeStruct((nzl, nc, ny, local_docs * half + 128), f32),
        scratch_shapes=[pltpu.VMEM((nc, half // 128 + 1, row_docs, 128), f32)],
        name="pair_table",
    )(positives, normalizers, probs, after)


def tile_body(q_ref, d_ref, n_ref, sent_ref, mine_ref, other_ref, dr_ref, nr_ref, w_ref):
    ny, nc, local_slots, width = d_ref.shape
    nzl, _, _, lanes = n_ref.shape
    lines = nc * ny
    nx, nzh, _, rows, _ = q_ref.shape
    half = nx * nzh * rows
    tokens = nzl * half
    local_docs = (lanes - 128) // half
    length = local_slots // local_docs
    me = lax.axis_index("c")
    for r, core in enumerate((me, 1 - me)):
        for y in range(ny):
            at = (r * ny + y) * local_slots
            dr_ref[at : at + local_slots, :] = d_ref[y, core]
        for j in range(nzl):
            nr_ref[j * lines + r * ny : j * lines + (r + 1) * ny, :] = n_ref[j, core]
    q = jnp.transpose(q_ref[...], (2, 0, 1, 3, 4)).reshape(tokens, width)
    column = lax.broadcasted_iota(jnp.int32, (128, local_docs * half), 1) // rows
    spread = (column == lax.broadcasted_iota(jnp.int32, (128, local_docs * half), 0)).astype(f32)
    signal = jnp.dot(
        nr_ref[:, local_docs * half :], spread, preferred_element_type=f32, precision=HIGHEST
    )
    for first_doc in range(0, lines * local_docs, GROUP):
        at = first_doc * length
        d = dr_ref[at : at + GROUP * length, :]
        s = lax.dot_general(d, q, (((1,), (1,)), ((), ())), preferred_element_type=f32)
        for k in range(GROUP):
            line, e = divmod(first_doc + k, local_docs)
            here = slice(e * half, (e + 1) * half)
            which = [j * lines + line for j in range(nzl)]
            z = jnp.concatenate([nr_ref[i : i + 1, here] for i in which], axis=1)
            p = jnp.concatenate([signal[i : i + 1, here] for i in which], axis=1)
            t = jnp.minimum(s[k * length : (k + 1) * length] * (SHARPNESS * LOG2E) - z, 0.0)
            w_ref[at + k * length : at + (k + 1) * length, :] = (jnp.exp2(t) * p).astype(bf16)
    w = w_ref[...]
    qg = lax.dot_general(dr_ref[...], w, (((0,), (0,)), ((), ())), preferred_element_type=f32).T
    most = jnp.max(jnp.max(jnp.abs(qg).reshape(-1, 8, width), axis=0), keepdims=True)
    top = jnp.broadcast_to(jnp.ceil(jnp.log2(jnp.maximum(most, 1e-30))), (1, width))
    qg = (qg * jnp.exp2(TOP - top)).reshape(nzl, nx, nzh, rows, width)
    for x in range(nx):
        for j in range(nzl):
            for zh in range(nzh):
                at = (zh * nzl + j) * rows
                sent_ref[x, at : at + rows, :] = qg[j, x, zh]
        sent_ref[x, nzh * nzl * rows :, :] = jnp.broadcast_to(top, (EXPONENT_ROWS, width))
    own = mine_ref.shape[0]
    mine_ref[...] = jnp.dot(w[:own], q, preferred_element_type=f32)
    other_ref[...] = jnp.dot(w[own:], q, preferred_element_type=f32)


def tile_gradients(q, d, n):
    nx, nzh, nzl, rows, width = q.shape
    ny, nc, local_slots, _ = d.shape
    slots = ny * nc * local_slots
    piece = nzh * nzl * rows
    vmem = pl.BlockSpec(memory_space=pltpu.VMEM)
    return pl.pallas_call(
        tile_body,
        in_specs=[vmem] * 3,
        out_specs=[vmem] * 3,
        out_shape=[
            jax.ShapeDtypeStruct((nx, piece + EXPONENT_ROWS, width), f32),
            jax.ShapeDtypeStruct((slots // nc, width), f32),
            jax.ShapeDtypeStruct((slots // nc, width), f32),
        ],
        scratch_shapes=[
            pltpu.VMEM((slots, width), bf16),
            pltpu.VMEM((nzl * nc * ny, n.shape[3]), f32),
            pltpu.VMEM((slots, nx * piece), bf16),
        ],
        name="pair_tile",
        compiler_params=pltpu.CompilerParams(vmem_limit_bytes=40 * MIB),
        cost_estimate=pl.CostEstimate(
            flops=6 * nx * piece * slots * width,
            bytes_accessed=8 * nx * piece * width,
            transcendentals=nx * piece * slots,
        ),
    )(q, d, n)


def exchange(x, axes):
    return lax.all_to_all(x, axes, split_axis=0, concat_axis=0, tiled=True)


def summed(sent, axes):
    got = exchange(sent, axes).astype(f32)
    tops = got[:, -EXPONENT_ROWS : 1 - EXPONENT_ROWS]
    return jnp.sum(got[:, :-EXPONENT_ROWS] * jnp.exp2(tops - TOP), axis=0), jnp.max(tops, axis=0)


def per_device(queries, documents, lengths, normalizers, probs, positives):
    sizes = tuple(lax.axis_size(a) for a in ("x", "zh", "c", "y", "zl"))
    nx, nzh, nc, ny, nzl = sizes
    nz = nzh * nzl
    rows, width = queries.shape
    length = documents.shape[0] // lengths.shape[0]

    copies, live_docs = first(nz, lengths, queries, documents)
    q = exchange(copies, RING).reshape(nz * rows, width)
    q = lax.all_gather(q, "x", tiled=True).reshape(nx, nzh, nzl, rows, width)

    d = lax.all_gather(live_docs, ("y", "c"), tiled=True)
    table = make_table(sizes, positives, normalizers, probs, d)
    table = exchange(table.reshape(nzl * nc, *table.shape[2:]), ("zl", "c")).reshape(table.shape)
    d = d.reshape(ny, nc, -1, width)

    sent, mine, other = tile_gradients(q, d, table)

    mine = (mine + lax.ppermute(other, "c", [(i, 1 - i) for i in range(nc)])).reshape(ny, -1, width)
    y = lax.axis_index("y")
    doc_grad = lax.dynamic_index_in_dim(mine, y, 0, keepdims=False)
    for k in range(1, ny):
        away = lax.dynamic_index_in_dim(mine, lax.rem(y + k, ny), 0, keepdims=False)
        doc_grad = doc_grad + lax.ppermute(away, "y", [(i, (i + k) % ny) for i in range(ny)])
    live = (jnp.arange(length, dtype=jnp.int32)[None, :] < lengths[:, None]).reshape(-1, 1)
    doc_grad = jnp.where(live, doc_grad, 0.0)

    total, top = summed(sent.astype(f16), "x")
    top = top + (nx - 1).bit_length()
    sent = (total * jnp.exp2(TOP - top)).reshape(nz, rows, width)
    sent = jnp.concatenate([sent, jnp.broadcast_to(top, (nz, EXPONENT_ROWS, width))], axis=1)
    query_grad, _ = summed(sent.astype(f16), RING)
    return query_grad, doc_grad


def solution(mesh):
    split = Mesh(mesh.devices.reshape(4, 2, 2, 4, 8), ("x", "zh", "c", "y", "zl"))
    return jax.shard_map(
        per_device,
        mesh=split,
        in_specs=(
            P((*QUERY_AXES, *DOC_AXES), None),
            P((*DOC_AXES, *QUERY_AXES), None),
            P((*DOC_AXES, *QUERY_AXES)),
            P(DOC_AXES, QUERY_AXES),
            P(QUERY_AXES, DOC_AXES),
            P(QUERY_AXES),
        ),
        out_specs=(P((*QUERY_AXES, *DOC_AXES), None), P((*DOC_AXES, *QUERY_AXES), None)),
        check_vma=False,
    )
```

```python
import jax
import jax.numpy as jnp
from jax import lax
from jax.experimental import pallas as pl
from jax.experimental.pallas import tpu as pltpu
from jax.sharding import Mesh
from jax.sharding import PartitionSpec as P

DOC_AXES = ("x", "zh", "c")
QUERY_AXES = ("y", "zl")
RING = ("zh", "zl")

SHARPNESS = 10.0
LOG2E = 1.4426950408889634
TOP = 14.0
EXPONENT_ROWS = 8
GROUP = 4
MIB = 1024 * 1024
f32, f16, bf16 = jnp.float32, jnp.float16, jnp.bfloat16
HIGHEST = lax.Precision.HIGHEST


def first_body(lengths_ref, queries_ref, docs_ref, copies_ref, d_ref):
    local_docs = lengths_ref.shape[0]
    length = docs_ref.shape[0] // local_docs
    for k in range(copies_ref.shape[0]):
        copies_ref[k] = queries_ref[...]
    for e in range(local_docs):
        block = docs_ref[e * length : (e + 1) * length, :].astype(f32)
        live = lax.broadcasted_iota(jnp.int32, block.shape, 0) < lengths_ref[e]
        d_ref[e * length : (e + 1) * length, :] = jnp.where(live, block, 0.0).astype(bf16)


def first(nz, lengths, queries, documents):
    smem, vmem = pl.BlockSpec(memory_space=pltpu.SMEM), pl.BlockSpec(memory_space=pltpu.VMEM)
    return pl.pallas_call(
        first_body,
        in_specs=[smem, vmem, vmem],
        out_specs=[vmem, vmem],
        out_shape=[
            jax.ShapeDtypeStruct((nz, *queries.shape), bf16),
            jax.ShapeDtypeStruct(documents.shape, bf16),
        ],
        name="first",
    )(lengths, queries, documents)


def table_body(nx, nzh, nc, ny, nzl, positives_ref, z_ref, probs_ref, after_ref, out_ref, t_ref):
    row_docs, row_tokens = z_ref.shape
    row_queries = probs_ref.shape[0]
    rows = row_tokens // row_queries
    local_docs = row_docs // (ny * nzl)
    groups = row_queries // nc
    half = groups * rows
    chunks = half // 128
    first_doc = ((lax.axis_index("x") * nzh + lax.axis_index("zh")) * nc + lax.axis_index("c")) * row_docs
    doc = first_doc + lax.broadcasted_iota(jnp.int32, probs_ref.shape, 1)
    query = lax.broadcasted_iota(jnp.int32, probs_ref.shape, 0)
    hit = jnp.zeros(probs_ref.shape, jnp.bool_)
    for i in range(row_queries):
        hit = hit | ((query == i) & (doc == positives_ref[i]))
    signal = probs_ref[...] - hit.astype(f32)

    z = z_ref[...] * LOG2E
    count = row_docs // local_docs
    for c in range(nc):
        columns = [z[:, (g * nc + c) * rows : (g * nc + c + 1) * rows] for g in range(groups)]
        columns = jnp.concatenate(columns, axis=1)
        one = (
            lax.broadcasted_iota(jnp.int32, (row_queries, 128), 0)
            == lax.broadcasted_iota(jnp.int32, (row_queries, 128), 1) * nc + c
        )
        turned = lax.dot_general(
            signal, one.astype(f32), (((0,), (0,)), ((), ())), preferred_element_type=f32, precision=HIGHEST
        )
        for k in range(chunks):
            t_ref[c, k] = columns[:, k * 128 : (k + 1) * 128]
        t_ref[c, chunks] = turned
        tail = jnp.zeros((count, 128), f32)
        for e in range(local_docs):
            lines = [t_ref.at[c, k][pl.ds(e, count, stride=local_docs), :] for k in range(chunks + 1)]
            for k in range(chunks):
                for y in range(ny):
                    at = e * half + k * 128
                    out_ref[:, c, y, at : at + 128] = lines[k][y * nzl : (y + 1) * nzl]
            tail = tail + (pltpu.roll(lines[chunks], e * groups, 1) if e else lines[chunks])
        for y in range(ny):
            out_ref[:, c, y, local_docs * half :] = tail[y * nzl : (y + 1) * nzl]


def make_table(sizes, positives, normalizers, probs, after):
    _, _, nc, ny, nzl = sizes
    row_docs, row_tokens = normalizers.shape
    half = row_tokens // nc
    local_docs = row_docs // (ny * nzl)
    smem, vmem = pl.BlockSpec(memory_space=pltpu.SMEM), pl.BlockSpec(memory_space=pltpu.VMEM)
    return pl.pallas_call(
        lambda *refs: table_body(*sizes, *refs),
        in_specs=[smem, vmem, vmem, pl.BlockSpec(memory_space=pl.ANY)],
        out_specs=vmem,
        out_shape=jax.ShapeDtypeStruct((nzl, nc, ny, local_docs * half + 128), f32),
        scratch_shapes=[pltpu.VMEM((nc, half // 128 + 1, row_docs, 128), f32)],
        name="pair_table",
    )(positives, normalizers, probs, after)


def tile_body(q_ref, d_ref, n_ref, sent_ref, mine_ref, other_ref, dr_ref, nr_ref, w_ref):
    ny, nc, local_slots, width = d_ref.shape
    nzl, _, _, lanes = n_ref.shape
    lines = nc * ny
    nx, nzh, _, rows, _ = q_ref.shape
    half = nx * nzh * rows
    tokens = nzl * half
    local_docs = (lanes - 128) // half
    length = local_slots // local_docs
    me = lax.axis_index("c")
    for r, core in enumerate((me, 1 - me)):
        for y in range(ny):
            at = (r * ny + y) * local_slots
            dr_ref[at : at + local_slots, :] = d_ref[y, core]
        for j in range(nzl):
            nr_ref[j * lines + r * ny : j * lines + (r + 1) * ny, :] = n_ref[j, core]
    q = jnp.transpose(q_ref[...], (2, 0, 1, 3, 4)).reshape(tokens, width)
    column = lax.broadcasted_iota(jnp.int32, (128, local_docs * half), 1) // rows
    spread = (column == lax.broadcasted_iota(jnp.int32, (128, local_docs * half), 0)).astype(f32)
    signal = jnp.dot(
        nr_ref[:, local_docs * half :], spread, preferred_element_type=f32, precision=HIGHEST
    )
    for first_doc in range(0, lines * local_docs, GROUP):
        at = first_doc * length
        d = dr_ref[at : at + GROUP * length, :]
        s = lax.dot_general(d, q, (((1,), (1,)), ((), ())), preferred_element_type=f32)
        for k in range(GROUP):
            line, e = divmod(first_doc + k, local_docs)
            here = slice(e * half, (e + 1) * half)
            which = [j * lines + line for j in range(nzl)]
            z = jnp.concatenate([nr_ref[i : i + 1, here] for i in which], axis=1)
            p = jnp.concatenate([signal[i : i + 1, here] for i in which], axis=1)
            t = jnp.minimum(s[k * length : (k + 1) * length] * (SHARPNESS * LOG2E) - z, 0.0)
            w_ref[at + k * length : at + (k + 1) * length, :] = (jnp.exp2(t) * p).astype(bf16)
        part = jnp.dot(w_ref[at : at + GROUP * length, :], q, preferred_element_type=f32)
        own = mine_ref.shape[0]
        if at < own:
            mine_ref[at : at + GROUP * length, :] = part
        else:
            other_ref[at - own : at - own + GROUP * length, :] = part
    w = w_ref[...]
    qg = lax.dot_general(dr_ref[...], w, (((0,), (0,)), ((), ())), preferred_element_type=f32).T
    most = jnp.max(jnp.max(jnp.abs(qg).reshape(-1, 8, width), axis=0), keepdims=True)
    top = jnp.broadcast_to(jnp.ceil(jnp.log2(jnp.maximum(most, 1e-30))), (1, width))
    qg = (qg * jnp.exp2(TOP - top)).reshape(nzl, nx, nzh, rows, width)
    for x in range(nx):
        for j in range(nzl):
            for zh in range(nzh):
                at = (zh * nzl + j) * rows
                sent_ref[x, at : at + rows, :] = qg[j, x, zh]
        sent_ref[x, nzh * nzl * rows :, :] = jnp.broadcast_to(top, (EXPONENT_ROWS, width))


def tile_gradients(q, d, n):
    nx, nzh, nzl, rows, width = q.shape
    ny, nc, local_slots, _ = d.shape
    slots = ny * nc * local_slots
    piece = nzh * nzl * rows
    vmem = pl.BlockSpec(memory_space=pltpu.VMEM)
    return pl.pallas_call(
        tile_body,
        in_specs=[vmem] * 3,
        out_specs=[vmem] * 3,
        out_shape=[
            jax.ShapeDtypeStruct((nx, piece + EXPONENT_ROWS, width), f32),
            jax.ShapeDtypeStruct((slots // nc, width), f32),
            jax.ShapeDtypeStruct((slots // nc, width), f32),
        ],
        scratch_shapes=[
            pltpu.VMEM((slots, width), bf16),
            pltpu.VMEM((nzl * nc * ny, n.shape[3]), f32),
            pltpu.VMEM((slots, nx * piece), bf16),
        ],
        name="pair_tile",
        compiler_params=pltpu.CompilerParams(vmem_limit_bytes=40 * MIB),
        cost_estimate=pl.CostEstimate(
            flops=6 * nx * piece * slots * width,
            bytes_accessed=8 * nx * piece * width,
            transcendentals=nx * piece * slots,
        ),
    )(q, d, n)


def exchange(x, axes):
    return lax.all_to_all(x, axes, split_axis=0, concat_axis=0, tiled=True)


def summed(sent, axes):
    got = exchange(sent, axes).astype(f32)
    tops = got[:, -EXPONENT_ROWS : 1 - EXPONENT_ROWS]
    return jnp.sum(got[:, :-EXPONENT_ROWS] * jnp.exp2(tops - TOP), axis=0), jnp.max(tops, axis=0)


def per_device(queries, documents, lengths, normalizers, probs, positives):
    sizes = tuple(lax.axis_size(a) for a in ("x", "zh", "c", "y", "zl"))
    nx, nzh, nc, ny, nzl = sizes
    nz = nzh * nzl
    rows, width = queries.shape
    length = documents.shape[0] // lengths.shape[0]

    copies, live_docs = first(nz, lengths, queries, documents)
    q = exchange(copies, RING).reshape(nz * rows, width)
    q = lax.all_gather(q, "x", tiled=True).reshape(nx, nzh, nzl, rows, width)

    d = lax.all_gather(live_docs, ("y", "c"), tiled=True)
    table = make_table(sizes, positives, normalizers, probs, d)
    table = exchange(table.reshape(nzl * nc, *table.shape[2:]), ("zl", "c")).reshape(table.shape)
    d = d.reshape(ny, nc, -1, width)

    sent, mine, other = tile_gradients(q, d, table)

    mine = (mine + lax.ppermute(other, "c", [(i, 1 - i) for i in range(nc)])).reshape(ny, -1, width)
    y = lax.axis_index("y")
    doc_grad = lax.dynamic_index_in_dim(mine, y, 0, keepdims=False)
    for k in range(1, ny):
        away = lax.dynamic_index_in_dim(mine, lax.rem(y + k, ny), 0, keepdims=False)
        doc_grad = doc_grad + lax.ppermute(away, "y", [(i, (i + k) % ny) for i in range(ny)])
    live = (jnp.arange(length, dtype=jnp.int32)[None, :] < lengths[:, None]).reshape(-1, 1)
    doc_grad = jnp.where(live, doc_grad, 0.0)

    total, top = summed(sent.astype(f16), "x")
    top = top + (nx - 1).bit_length()
    sent = (total * jnp.exp2(TOP - top)).reshape(nz, rows, width)
    sent = jnp.concatenate([sent, jnp.broadcast_to(top, (nz, EXPONENT_ROWS, width))], axis=1)
    query_grad, _ = summed(sent.astype(f16), RING)
    return query_grad, doc_grad


def solution(mesh):
    split = Mesh(mesh.devices.reshape(4, 2, 2, 4, 8), ("x", "zh", "c", "y", "zl"))
    return jax.shard_map(
        per_device,
        mesh=split,
        in_specs=(
            P((*QUERY_AXES, *DOC_AXES), None),
            P((*DOC_AXES, *QUERY_AXES), None),
            P((*DOC_AXES, *QUERY_AXES)),
            P(DOC_AXES, QUERY_AXES),
            P(QUERY_AXES, DOC_AXES),
            P(QUERY_AXES),
        ),
        out_specs=(P((*QUERY_AXES, *DOC_AXES), None), P((*DOC_AXES, *QUERY_AXES), None)),
        check_vma=False,
    )
```
